512 devices in a mesh: space: 32 (over z, core), member: 16 (over y, x).
Axes of the slice: x: 4, y: 4, z: 16, core: 2. Of those that a mesh axis runs over, the one named last changes fastest.
Arguments:
- ensemble: bfloat16 [524288, 256], P('space', 'member'), may hold values from -20 to 20
- operator_blocks: bfloat16 [2048, 8, 128, 128], P('space')
- block_columns: int32 [2048, 8], P('space'), may hold values from 0 to 4095, as said below
- observed: float32 [262144], P('space')
- error_scale: float32 [262144], P('space'), as said below
Outputs:
- analysis: bfloat16 [524288, 256], P('space', 'member')
The draws below stay inside these ranges and needn't reach their ends.
Inputs may be any that keep to these rules, and one draw needn't show every extreme that they name: `block_columns`: block row r reads state blocks 128 * (r // 64) - 1 + j modulo 4096, 0 <= j <= 129; its first entry has j = 0 and its second j = 129. `error_scale`: Positive.
All inputs are finite; a program needn't handle non-finite values.
Results may differ from the reference program's by a relative error of at most 0.0059.
Values may be sent and summed in bfloat16 or wider, within the bound.
No kernel may reach another device: no remote copies, remote signals or barrier semaphores. Data moves between devices by JAX's collectives and lax.ppermute only.
A program may use at most 128 MiB of HBM per device.

```python
import math
import jax
import jax.numpy as jnp
from jax import lax

M = 256
B = 128
K = 8
SB_DEV = 128
OB_DEV = 64
ROWS_DEV = 16384
OBS_DEV = 8192
SBLOCKS = 4096
OBLOCKS = 2048
NSTATE = 524288
NOBS = 262144
N_SPACE = 32


def draw_ensemble(key, part):
    key = jax.random.fold_in(key, 11)
    center = 0.5 * jax.random.truncated_normal(jax.random.fold_in(key, 1), -4.0, 4.0, (NSTATE, 1), jnp.float32)
    spreads = jnp.exp(jax.random.uniform(jax.random.fold_in(key, 2), (1, M), jnp.float32, math.log(0.3), math.log(3.0)))
    noise = jax.random.truncated_normal(jax.random.fold_in(key, 3), -4.0, 4.0, (NSTATE, M), jnp.float32)
    return (center + spreads * noise).astype(jnp.bfloat16)


def draw_operator_blocks(key, part):
    key = jax.random.fold_in(key, 17)
    values = jax.random.truncated_normal(key, -4.0, 4.0, (OBLOCKS, K, B, B), jnp.float32)
    slot_ids = jnp.arange(K, dtype=jnp.int32)
    slot_scale = jnp.where(slot_ids < 2, 3.0, 1.0).astype(jnp.float32)
    norm = 1.0 / math.sqrt(B * (18.0 + (K - 2)))
    return (values * (slot_scale * norm)[None, :, None, None]).astype(jnp.bfloat16)


def draw_block_columns(key, part):
    key = jax.random.fold_in(key, 23)
    row_ids = jnp.arange(OBLOCKS, dtype=jnp.int32)
    owners = row_ids // OB_DEV
    offsets = jax.random.randint(key, (OBLOCKS, K), 0, SB_DEV + 2, jnp.int32)
    slot_ids = jnp.arange(K, dtype=jnp.int32)[None, :]
    offsets = jnp.where(slot_ids == 0, 0, jnp.where(slot_ids == 1, SB_DEV + 1, offsets))
    return jnp.mod(owners[:, None] * SB_DEV - 1 + offsets, SBLOCKS).astype(jnp.int32)


def draw_error_scale(key, part):
    key = jax.random.fold_in(key, 31)
    spread_base = math.sqrt(NOBS / M)
    shard_count = NOBS // OBS_DEV
    shard_ids = (jnp.arange(NOBS, dtype=jnp.int32) // OBS_DEV).astype(jnp.float32)
    trend = jnp.exp(-0.5 * math.log(3.0) * shard_ids / max(shard_count - 1, 1))
    factor = jnp.exp(jax.random.uniform(key, (NOBS,), jnp.float32, math.log(0.5), math.log(2.0)))
    return (spread_base * factor * trend).astype(jnp.float32)


def draw_observed(key, part):
    key = jax.random.fold_in(key, 37)
    spread_base = 2.0 * math.sqrt(NOBS / M)
    values = jax.random.truncated_normal(key, -4.0, 4.0, (NOBS,), jnp.float32)
    return (spread_base * values).astype(jnp.float32)


def setup_inputs(seed: int = 0) -> dict:
    key_of = jax.random.split(jax.random.key(seed), 6)
    return {
        "ensemble": draw_ensemble(jax.random.fold_in(key_of[5], 71), 0),
        "operator_blocks": draw_operator_blocks(jax.random.fold_in(key_of[5], 71), 0),
        "block_columns": draw_block_columns(jax.random.fold_in(key_of[5], 71), 0),
        "observed": draw_observed(jax.random.fold_in(key_of[5], 71), 0),
        "error_scale": draw_error_scale(jax.random.fold_in(key_of[5], 71), 0),
    }


def reference(ensemble, operator_blocks, block_columns, observed, error_scale):
    mean_state = lax.optimization_barrier(jnp.sum(ensemble, axis=1, dtype=jnp.float32)) / M
    state_blocks = ensemble.reshape(SBLOCKS, B, M)

    def predict_group(group):
        weights, columns = group
        picked = state_blocks[columns]
        return jnp.einsum('okij,okjm->oim', weights.astype(jnp.float32), picked.astype(jnp.float32))
    predicted = lax.map(predict_group, (operator_blocks.reshape(N_SPACE, OB_DEV, K, B, B), block_columns.reshape(N_SPACE, OB_DEV, K))).reshape(NOBS, M)
    mean_pred = lax.optimization_barrier(jnp.sum(predicted, axis=1)) / M
    root_scale = math.sqrt(M - 1)
    whitened = (predicted - mean_pred[:, None]) / (error_scale * root_scale)[:, None]
    departure = (observed - mean_pred) / (error_scale * root_scale)
    identity = jnp.eye(M, dtype=jnp.float32)
    gram_matrix = identity + jnp.dot(whitened.T, whitened, precision=lax.Precision.HIGHEST)
    cross_term = jnp.dot(departure, whitened, precision=lax.Precision.HIGHEST)
    lower_factor = jnp.linalg.cholesky(gram_matrix)
    weight_mean = jax.scipy.linalg.cho_solve((lower_factor, True), cross_term)
    inverse_lower = jax.scipy.linalg.solve_triangular(lower_factor, identity, lower=True)
    transform = (inverse_lower.T + weight_mean[:, None]).astype(jnp.bfloat16)

    def analyse_group(group):
        members, center = group
        anomalies = (members.astype(jnp.float32) - center[:, None]).astype(jnp.bfloat16)
        return (center[:, None] + jnp.dot(anomalies.astype(jnp.float32), transform.astype(jnp.float32), preferred_element_type=jnp.float32)).astype(jnp.bfloat16)
    analysis = lax.map(analyse_group, (ensemble.reshape(N_SPACE, ROWS_DEV, M), mean_state.reshape(N_SPACE, ROWS_DEV))).reshape(NSTATE, M)
    return analysis
```

```python
import functools
import math

import jax
import jax.numpy as jnp
from jax import lax
from jax.experimental import pallas as pl
from jax.experimental.pallas import tpu as pltpu
from jax.sharding import Mesh
from jax.sharding import PartitionSpec as P

F32, BF16 = jnp.float32, jnp.bfloat16
HIGHEST = lax.Precision.HIGHEST
NT = (((1,), (1,)), ((), ()))
TN = (((0,), (0,)), ((), ()))
PLANE = ("core", "y", "x")
MEMBER = ("y", "x")
SPACE = ("z", "core")


def predict_kernel(group, cols_ref, ens_ref, left_ref, right_ref, ops_ref, out_ref, blocks):
    step = pl.program_id(0)
    count = ens_ref.shape[1] // 128

    @pl.when(step == 0)
    def _():
        blocks[0] = left_ref[...]
        blocks[count + 1] = right_ref[...]
        for j in range(count):
            blocks[j + 1] = ens_ref[:, 128 * j : 128 * (j + 1)]

    for o in range(group):
        picked = jnp.concatenate([blocks[cols_ref[step * group + o, k]] for k in range(8)], axis=1)
        weights = jnp.concatenate([ops_ref[o, k] for k in range(8)], axis=1)
        part = lax.dot_general(weights, picked, NT, preferred_element_type=F32)
        out_ref[:, 128 * o : 128 * (o + 1)] = part.T


def predict(cols, ens_t, left, right, ops, group=8):
    members, rows = ens_t.shape
    oblocks = ops.shape[0]
    whole = lambda shape: pl.BlockSpec(shape, lambda i, c: (0, 0))
    return pl.pallas_call(
        functools.partial(predict_kernel, group),
        out_shape=jax.ShapeDtypeStruct((members, oblocks * 128), F32),
        grid_spec=pltpu.PrefetchScalarGridSpec(
            num_scalar_prefetch=1,
            grid=(oblocks // group,),
            in_specs=[
                whole(ens_t.shape),
                whole(left.shape),
                whole(right.shape),
                pl.BlockSpec((group, 8, 128, 128), lambda i, c: (i, 0, 0, 0)),
            ],
            out_specs=pl.BlockSpec((members, group * 128), lambda i, c: (0, i)),
            scratch_shapes=[pltpu.VMEM((rows // 128 + 2, members, 128), BF16)],
        ),
        compiler_params=pltpu.CompilerParams(vmem_limit_bytes=24 * 2**20),
        cost_estimate=pl.CostEstimate(flops=2 * ops.size * members, bytes_accessed=2 * ops.size, transcendentals=0),
    )(cols, ens_t, left, right, ops)


def gram_kernel(pred_ref, obs_ref, err_ref, out_ref):
    total, half = pred_ref.shape[0], pred_ref.shape[0] // 2
    pred = pred_ref[...]
    mean = jnp.sum(pred, axis=0, keepdims=True) / total
    scale = err_ref[...] * math.sqrt(total - 1)
    white = (pred - mean) / scale
    departure = (obs_ref[...] - mean) / scale
    row = lax.broadcasted_iota(jnp.int32, (half, white.shape[1]), 0)
    first = jnp.where(row == 0, departure, 0.0)
    second = jnp.where(row == 1, departure, 0.0)
    top, low = white[:half], white[half:]
    dot = functools.partial(lax.dot_general, dimension_numbers=NT, precision=HIGHEST, preferred_element_type=F32)
    out_ref[:half, :half] = dot(top, top)
    out_ref[:half, half:] = dot(top, first) + dot(low, second)
    out_ref[half:, :] = dot(low, white)


def gram(pred, obs, err):
    total = pred.shape[0]
    return pl.pallas_call(
        gram_kernel,
        out_shape=jax.ShapeDtypeStruct((total, total), F32),
        compiler_params=pltpu.CompilerParams(vmem_limit_bytes=24 * 2**20),
    )(pred, obs, err)


WIDE = 32


def spread(column):
    return jnp.broadcast_to(column, (8, 128))


def eliminate(panel, col0):
    groups = WIDE // 8
    sub = lax.broadcasted_iota(jnp.int32, (8, 128), 0)
    tile = col0 // 128
    lanes = lax.broadcasted_iota(jnp.int32, (8, 128), 1) + 128 * tile
    tiles = panel[0].shape[1] // 128
    panel = [[p[:, 128 * t : 128 * (t + 1)] for t in range(tiles)] for p in panel]
    out = []
    for q in range(groups):
        start = col0 + 8 * q
        at = start - 128 * tile
        coef = [[None if g < q else spread(panel[g][tile][:, at + c : at + c + 1]) for g in range(groups)] for c in range(8)]
        pivots = jnp.ones((8, 128), F32)
        for j in range(8):
            pivot = spread(coef[j][q][j : j + 1, :])
            pivots = jnp.where(sub == j, pivot, pivots)
            ratio = 1.0 / pivot
            ahead = [spread(coef[c][q][j : j + 1, :]) for c in range(8)]
            for g in range(q, groups):
                times = coef[j][g] * ratio
                if g == q:
                    times = jnp.where(sub > j, times, 0.0)
                for c in range(8):
                    if c == j:
                        coef[c][g] = jnp.where(sub == j, 1.0, -times) if g == q else -times
                    else:
                        coef[c][g] = coef[c][g] - times * ahead[c]
        inside = (lanes >= start) & (lanes < start + 8)
        unit = jnp.where(lanes - start == sub, 1.0, 0.0)
        base = [jnp.where(inside, unit, panel[q][t]) if t == tile else panel[q][t] for t in range(tiles)]
        root = lax.rsqrt(pivots)
        rows = [[spread(base[t][c : c + 1, :]) for t in range(tiles)] for c in range(8)]
        low = [jnp.where(sub >= c, coef[c][q], 0.0) for c in range(8)]
        out.append([sum(low[c] * rows[c][t] for c in range(8)) * root for t in range(tiles)])
        for g in range(q + 1, groups):
            for t in range(tiles):
                here = jnp.where(inside, 0.0, panel[g][t]) if t == tile else panel[g][t]
                panel[g][t] = here + sum(coef[c][g] * rows[c][t] for c in range(8))
    return jnp.concatenate([jnp.concatenate(o, axis=1) for o in out], axis=0)


def transform_kernel(mine_ref, gram_ref, out_ref, a):
    total = gram_ref.shape[0]
    half = total // 2
    row = lax.broadcasted_iota(jnp.int32, (total, total), 0)
    col = lax.broadcasted_iota(jnp.int32, (total, total), 1)
    given = gram_ref[...]
    extra = given[:half, half:]
    cross = jnp.concatenate([extra[:, 0:1], extra[:, 1:2]], axis=0)
    mirror = given[half:, :half].T
    full = jnp.concatenate([jnp.concatenate([given[:half, :half], mirror], axis=1), given[half:, :]], axis=0)
    a[...] = full + jnp.where(row == col, 1.0, 0.0)
    for s in range(total // WIDE):
        r0, r1 = WIDE * s, WIDE * (s + 1)
        done = eliminate([a[r0 + 8 * g : r0 + 8 * (g + 1), :] for g in range(WIDE // 8)], r0)
        a[r0:r1, :] = done
        if r1 < total:
            above = (col[r0:r1] < r1) & (col[r0:r1] > row[r0:r1])
            kept = jnp.where(above, 0.0, done)
            update = lax.dot_general(done, kept, TN, precision=HIGHEST, preferred_element_type=F32)
            block = (col[r1:] >= r0) & (col[r1:] < r1)
            a[r1:, :] = jnp.where(block, 0.0, a[r1:, :]) - update[r1:, :]
    inverse = jnp.where(col <= row, a[...], 0.0)
    a[...] = inverse
    solved = jnp.sum(inverse * cross.T, axis=1, keepdims=True)
    weight = jnp.sum(inverse * solved, axis=0, keepdims=True)
    mine = a[pl.ds(pl.multiple_of(mine_ref[0] * 16, 16), 16), :]
    rounded = (mine + weight).astype(BF16).astype(F32)
    centred = rounded - jnp.sum(rounded, axis=1, keepdims=True) / total + 1.0 / total
    high = centred.astype(BF16)
    out_ref[:16] = high
    out_ref[16:] = (centred - high.astype(F32)).astype(BF16)


def transform(mine, gram_sum):
    total = gram_sum.shape[0]
    return pl.pallas_call(
        transform_kernel,
        out_shape=jax.ShapeDtypeStruct((32, total), BF16),
        in_specs=[pl.BlockSpec(memory_space=pltpu.SMEM), pl.BlockSpec(memory_space=pltpu.VMEM)],
        out_specs=pl.BlockSpec(memory_space=pltpu.VMEM),
        scratch_shapes=[pltpu.VMEM((total, total), F32)],
        compiler_params=pltpu.CompilerParams(vmem_limit_bytes=24 * 2**20),
    )(mine, gram_sum)


def update_kernel(left_ref, all_ref, out_ref):
    both = jnp.dot(left_ref[...], all_ref[...], preferred_element_type=F32)
    out_ref[...] = (both[:16] + both[16:]).astype(BF16)


def update(left, everyone, width=2048):
    total, rows = everyone.shape
    return pl.pallas_call(
        update_kernel,
        out_shape=jax.ShapeDtypeStruct((16, rows), BF16),
        grid=(rows // width,),
        in_specs=[pl.BlockSpec(left.shape, lambda i: (0, 0)), pl.BlockSpec((total, width), lambda i: (0, i))],
        out_specs=pl.BlockSpec((16, width), lambda i: (0, i)),
        compiler_params=pltpu.CompilerParams(vmem_limit_bytes=24 * 2**20),
        cost_estimate=pl.CostEstimate(flops=64 * total * rows, bytes_accessed=2 * total * rows, transcendentals=0),
    )(left, everyone)


def to_all(x, axes, count):
    return lax.all_to_all(jnp.broadcast_to(x[None], (count,) + x.shape), axes, 0, 0, tiled=True)


def local(ensemble, operator_blocks, block_columns, observed, error_scale):
    ens_t = ensemble.T
    members, rows = ens_t.shape
    space_count = lax.axis_size(SPACE)
    member_count = lax.axis_size(MEMBER)
    plane_count = lax.axis_size(PLANE)
    z_count = lax.axis_size("z")
    total = members * member_count
    space_index = lax.axis_index(SPACE)
    member_index = lax.axis_index(MEMBER)
    everyone = lax.all_gather(ens_t, MEMBER, axis=0, tiled=True)
    left = lax.ppermute(ens_t[:, -128:], SPACE, [(i, (i + 1) % space_count) for i in range(space_count)])
    right = lax.ppermute(ens_t[:, :128], SPACE, [((i + 1) % space_count, i) for i in range(space_count)])
    state_local = rows // 128
    cols = jnp.mod(block_columns - space_index * state_local + 1, state_local * space_count)
    predicted = predict(cols, ens_t, left, right, operator_blocks)
    predicted = lax.all_to_all(predicted, MEMBER, 1, 0, tiled=True)
    width = predicted.shape[1]
    obs = lax.dynamic_slice_in_dim(observed, member_index * width, width)[None]
    err = lax.dynamic_slice_in_dim(error_scale, member_index * width, width)[None]
    part = gram(predicted, obs, err).reshape(plane_count, -1, total)
    part = jnp.sum(lax.all_to_all(part, PLANE, 0, 0, tiled=True), axis=0)
    part = jnp.sum(to_all(part, "z", z_count), axis=0)
    gram_sum = to_all(part, PLANE, plane_count).reshape(total, total)
    mine = transform(member_index.astype(jnp.int32).reshape(1), gram_sum)
    return update(mine, everyone).T


def solution(mesh):
    fine = Mesh(mesh.devices.reshape(16, 2, 4, 4), ("z", "core", "y", "x"))
    in_specs = (P(SPACE, MEMBER), P(SPACE, None, None, None), P(SPACE, None), P(SPACE), P(SPACE))
    return jax.shard_map(local, mesh=fine, in_specs=in_specs, out_specs=P(SPACE, MEMBER), check_vma=False)
```

```python
import functools
import math

import jax
import jax.numpy as jnp
from jax import lax
from jax.experimental import pallas as pl
from jax.experimental.pallas import tpu as pltpu
from jax.sharding import Mesh
from jax.sharding import PartitionSpec as P

F32, BF16 = jnp.float32, jnp.bfloat16
HIGHEST = lax.Precision.HIGHEST
NT = (((1,), (1,)), ((), ()))
TN = (((0,), (0,)), ((), ()))
PLANE = ("core", "y", "x")
MEMBER = ("y", "x")
SPACE = ("z", "core")


def predict_kernel(cols_ref, ens_ref, left_ref, right_ref, ops_ref, out_ref, state, weights, state_sem, sems):
    parts, members, width = out_ref.shape
    group = width // 128
    rows = ens_ref.shape[1]

    def fetch(c):
        return pltpu.make_async_copy(ops_ref.at[pl.ds(c * group, group)], weights.at[pl.ds(c * group, group)], sems.at[c])

    inner = pltpu.make_async_copy(ens_ref, state.at[:, pl.ds(128, rows)], state_sem)
    inner.start()
    for c in range(4):
        fetch(c).start()
    state[:, :128] = left_ref[...]
    state[:, rows + 128 :] = right_ref[...]
    inner.wait()

    def body(c, carry):
        fetch(c).wait()

        @pl.when(c + 4 < parts)
        def _():
            fetch(c + 4).start()

        for o in range(group):
            block = c * group + o
            picked = [state[:, pl.ds(pl.multiple_of(cols_ref[block, k] * 128, 128), 128)] for k in range(8)]
            rows_of = [weights[block, k] for k in range(8)]
            out_ref[c, :, 128 * o : 128 * (o + 1)] = lax.dot_general(
                jnp.concatenate(picked, axis=1), jnp.concatenate(rows_of, axis=1), NT, preferred_element_type=F32
            )
        return carry

    lax.fori_loop(0, parts, body, 0)


def predict(cols, ens_t, left, right, ops, parts):
    members, rows = ens_t.shape
    oblocks = ops.shape[0]
    anywhere, inside = pl.BlockSpec(memory_space=pl.ANY), pl.BlockSpec(memory_space=pltpu.VMEM)
    return pl.pallas_call(
        predict_kernel,
        out_shape=jax.ShapeDtypeStruct((parts, members, oblocks * 128 // parts), F32),
        in_specs=[pl.BlockSpec(memory_space=pltpu.SMEM), anywhere, inside, inside, anywhere],
        out_specs=inside,
        scratch_shapes=[
            pltpu.VMEM((members, rows + 256), BF16),
            pltpu.VMEM(ops.shape, BF16),
            pltpu.SemaphoreType.DMA,
            pltpu.SemaphoreType.DMA((parts,)),
        ],
        compiler_params=pltpu.CompilerParams(vmem_limit_bytes=50 * 2**20),
        cost_estimate=pl.CostEstimate(flops=2 * ops.size * members, bytes_accessed=2 * ops.size, transcendentals=0),
    )(cols, ens_t, left, right, ops)


def gram_kernel(pred_ref, obs_ref, err_ref, out_ref):
    total, half = pred_ref.shape[0], pred_ref.shape[0] // 2
    pred = pred_ref[...]
    mean = jnp.sum(pred, axis=0, keepdims=True) / total
    scale = err_ref[...] * math.sqrt(total - 1)
    white = (pred - mean) / scale
    departure = (obs_ref[...] - mean) / scale
    row = lax.broadcasted_iota(jnp.int32, (half, white.shape[1]), 0)
    first = jnp.where(row == 0, departure, 0.0)
    second = jnp.where(row == 1, departure, 0.0)
    top, low = white[:half], white[half:]
    dot = functools.partial(lax.dot_general, dimension_numbers=NT, precision=HIGHEST, preferred_element_type=F32)
    out_ref[:half, :half] = dot(top, top)
    out_ref[:half, half:] = dot(top, first) + dot(low, second)
    out_ref[half:, :] = dot(low, white)


def gram(pred, obs, err):
    total = pred.shape[0]
    return pl.pallas_call(
        gram_kernel,
        out_shape=jax.ShapeDtypeStruct((total, total), F32),
        compiler_params=pltpu.CompilerParams(vmem_limit_bytes=16 * 2**20),
    )(pred, obs, err)


WIDE = 32


def spread(column):
    return jnp.broadcast_to(column, (8, 128))


def eliminate(panel, col0):
    groups = WIDE // 8
    sub = lax.broadcasted_iota(jnp.int32, (8, 128), 0)
    tile = col0 // 128
    lanes = lax.broadcasted_iota(jnp.int32, (8, 128), 1) + 128 * tile
    tiles = panel[0].shape[1] // 128
    panel = [[p[:, 128 * t : 128 * (t + 1)] for t in range(tiles)] for p in panel]
    out = []
    for q in range(groups):
        start = col0 + 8 * q
        at = start - 128 * tile
        coef = [[None if g < q else spread(panel[g][tile][:, at + c : at + c + 1]) for g in range(groups)] for c in range(8)]
        pivots = jnp.ones((8, 128), F32)
        for j in range(8):
            pivot = spread(coef[j][q][j : j + 1, :])
            pivots = jnp.where(sub == j, pivot, pivots)
            ratio = 1.0 / pivot
            ahead = [spread(coef[c][q][j : j + 1, :]) for c in range(8)]
            for g in range(q, groups):
                times = coef[j][g] * ratio
                if g == q:
                    times = jnp.where(sub > j, times, 0.0)
                for c in range(8):
                    if c == j:
                        coef[c][g] = jnp.where(sub == j, 1.0, -times) if g == q else -times
                    else:
                        coef[c][g] = coef[c][g] - times * ahead[c]
        inside = (lanes >= start) & (lanes < start + 8)
        unit = jnp.where(lanes - start == sub, 1.0, 0.0)
        base = [jnp.where(inside, unit, panel[q][t]) if t == tile else panel[q][t] for t in range(tiles)]
        root = lax.rsqrt(pivots)
        rows = [[spread(base[t][c : c + 1, :]) for t in range(tiles)] for c in range(8)]
        low = [jnp.where(sub >= c, coef[c][q], 0.0) for c in range(8)]
        out.append([sum(low[c] * rows[c][t] for c in range(8)) * root for t in range(tiles)])
        for g in range(q + 1, groups):
            for t in range(tiles):
                here = jnp.where(inside, 0.0, panel[g][t]) if t == tile else panel[g][t]
                panel[g][t] = here + sum(coef[c][g] * rows[c][t] for c in range(8))
    return jnp.concatenate([jnp.concatenate(o, axis=1) for o in out], axis=0)


def transform_kernel(gram_ref, ens_ref, out_ref, a):
    total = gram_ref.shape[0]
    half = total // 2
    row = lax.broadcasted_iota(jnp.int32, (total, total), 0)
    col = lax.broadcasted_iota(jnp.int32, (total, total), 1)
    given = gram_ref[...]
    extra = given[:half, half:]
    cross = jnp.concatenate([extra[:, 0:1], extra[:, 1:2]], axis=0)
    mirror = given[half:, :half].T
    full = jnp.concatenate([jnp.concatenate([given[:half, :half], mirror], axis=1), given[half:, :]], axis=0)
    a[...] = full + jnp.where(row == col, 1.0, 0.0)
    for s in range(total // WIDE):
        r0, r1 = WIDE * s, WIDE * (s + 1)
        done = eliminate([a[r0 + 8 * g : r0 + 8 * (g + 1), :] for g in range(WIDE // 8)], r0)
        a[r0:r1, :] = done
        if r1 < total:
            above = (col[r0:r1] < r1) & (col[r0:r1] > row[r0:r1])
            kept = jnp.where(above, 0.0, done)
            update = lax.dot_general(done, kept, TN, precision=HIGHEST, preferred_element_type=F32)
            block = (col[r1:] >= r0) & (col[r1:] < r1)
            a[r1:, :] = jnp.where(block, 0.0, a[r1:, :]) - update[r1:, :]
    inverse = jnp.where(col <= row, a[...], 0.0)
    a[...] = inverse
    solved = jnp.sum(inverse * cross.T, axis=1, keepdims=True)
    weight = jnp.sum(inverse * solved, axis=0, keepdims=True)
    rounded = (inverse + weight).astype(BF16).astype(F32)
    centred = rounded - jnp.sum(rounded, axis=1, keepdims=True) / total + 1.0 / total
    high = centred.astype(BF16)
    rest = (centred - high.astype(F32)).astype(BF16)
    states = ens_ref[...]
    both = jnp.dot(high, states, preferred_element_type=F32) + jnp.dot(rest, states, preferred_element_type=F32)
    out_ref[...] = both.astype(BF16)


def transform(gram_sum, states):
    total = gram_sum.shape[0]
    return pl.pallas_call(
        transform_kernel,
        out_shape=jax.ShapeDtypeStruct(states.shape, BF16),
        in_specs=[pl.BlockSpec(memory_space=pltpu.VMEM)] * 2,
        out_specs=pl.BlockSpec(memory_space=pltpu.VMEM),
        scratch_shapes=[pltpu.VMEM((total, total), F32)],
        compiler_params=pltpu.CompilerParams(vmem_limit_bytes=16 * 2**20),
    )(gram_sum, states)


def to_all(x, axes, count):
    return lax.all_to_all(jnp.broadcast_to(x[None], (count,) + x.shape), axes, 0, 0, tiled=True)


def local(ensemble, operator_blocks, block_columns, observed, error_scale):
    ens_t = ensemble.T
    members, rows = ens_t.shape
    space_count = lax.axis_size(SPACE)
    member_count = lax.axis_size(MEMBER)
    plane_count = lax.axis_size(PLANE)
    z_count = lax.axis_size("z")
    total = members * member_count
    space_index = lax.axis_index(SPACE)
    member_index = lax.axis_index(MEMBER)
    width = rows // member_count
    states = ens_t.reshape(members, member_count, width).transpose(1, 0, 2)
    states = lax.all_to_all(states, MEMBER, 0, 0, tiled=True)
    left = lax.ppermute(ens_t[:, -128:], SPACE, [(i, (i + 1) % space_count) for i in range(space_count)])
    right = lax.ppermute(ens_t[:, :128], SPACE, [((i + 1) % space_count, i) for i in range(space_count)])
    state_local = rows // 128
    cols = jnp.mod(block_columns - space_index * state_local + 1, state_local * space_count)
    predicted = predict(cols, ens_t, left, right, operator_blocks, member_count)
    predicted, states = lax.optimization_barrier((predicted, states))
    predicted = lax.all_to_all(predicted, MEMBER, 0, 0, tiled=True).reshape(total, -1)
    count = predicted.shape[1]
    obs = lax.dynamic_slice_in_dim(observed, member_index * count, count)[None]
    err = lax.dynamic_slice_in_dim(error_scale, member_index * count, count)[None]
    part = gram(predicted, obs, err).reshape(plane_count, -1, total)
    part = jnp.sum(lax.all_to_all(part, PLANE, 0, 0, tiled=True), axis=0)
    part = jnp.sum(to_all(part, "z", z_count), axis=0)
    gram_sum = to_all(part, PLANE, plane_count).reshape(total, total)
    analysis = transform(gram_sum, states.reshape(total, width)).reshape(member_count, members, width)
    analysis = lax.all_to_all(analysis, MEMBER, 0, 0, tiled=True)
    return analysis.transpose(1, 0, 2).reshape(members, rows).T


def solution(mesh):
    fine = Mesh(mesh.devices.reshape(16, 2, 4, 4), ("z", "core", "y", "x"))
    in_specs = (P(SPACE, MEMBER), P(SPACE, None, None, None), P(SPACE, None), P(SPACE), P(SPACE))
    return jax.shard_map(local, mesh=fine, in_specs=in_specs, out_specs=P(SPACE, MEMBER), check_vma=False)
```

```python
import functools
import math

import jax
import jax.numpy as jnp
from jax import lax
from jax.experimental import pallas as pl
from jax.experimental.pallas import tpu as pltpu
from jax.sharding import Mesh
from jax.sharding import PartitionSpec as P

F32, BF16 = jnp.float32, jnp.bfloat16
HIGHEST = lax.Precision.HIGHEST
NT = (((1,), (1,)), ((), ()))
TN = (((0,), (0,)), ((), ()))
PLANE = ("core", "y", "x")
MEMBER = ("y", "x")
SPACE = ("z", "core")


def predict_kernel(cols_ref, ens_ref, left_ref, right_ref, ops_ref, out_ref, state, weights, state_sem, sems):
    parts = out_ref.shape[0]
    rows = ens_ref.shape[1]
    group = ops_ref.shape[0] // parts
    width, share = 128 * group, rows // parts

    def fetch(c):
        return pltpu.make_async_copy(ops_ref.at[pl.ds(c * group, group)], weights.at[pl.ds(c * group, group)], sems.at[c])

    inner = pltpu.make_async_copy(ens_ref, state.at[:, pl.ds(128, rows)], state_sem)
    inner.start()
    for c in range(4):
        fetch(c).start()
    state[:, :128] = left_ref[...]
    state[:, rows + 128 :] = right_ref[...]
    inner.wait()

    def body(c, carry):
        fetch(c).wait()

        @pl.when(c + 4 < parts)
        def _():
            fetch(c + 4).start()

        for o in range(group):
            block = c * group + o
            picked = [state[:, pl.ds(pl.multiple_of(cols_ref[block, k] * 128, 128), 128)] for k in range(8)]
            rows_of = [weights[block, k] for k in range(8)]
            value = lax.dot_general(
                jnp.concatenate(picked, axis=1), jnp.concatenate(rows_of, axis=1), NT, preferred_element_type=F32
            )
            high = value.astype(BF16)
            out_ref[c, :, 128 * o : 128 * (o + 1)] = high
            out_ref[c, :, width + 128 * o : width + 128 * (o + 1)] = (value - high.astype(F32)).astype(BF16)
        out_ref[c, :, 2 * width :] = state[:, pl.ds(pl.multiple_of(128 + c * share, 128), share)]
        return carry

    lax.fori_loop(0, parts, body, 0)


def predict(cols, ens_t, left, right, ops, parts):
    members, rows = ens_t.shape
    oblocks = ops.shape[0]
    outside, inside = pl.BlockSpec(memory_space=pltpu.HBM), pl.BlockSpec(memory_space=pltpu.VMEM)
    return pl.pallas_call(
        predict_kernel,
        out_shape=jax.ShapeDtypeStruct((parts, members, (2 * oblocks * 128 + rows) // parts), BF16),
        in_specs=[pl.BlockSpec(memory_space=pltpu.SMEM), outside, inside, inside, outside],
        out_specs=inside,
        scratch_shapes=[
            pltpu.VMEM((members, rows + 256), BF16),
            pltpu.VMEM(ops.shape, BF16),
            pltpu.SemaphoreType.DMA,
            pltpu.SemaphoreType.DMA((parts,)),
        ],
        compiler_params=pltpu.CompilerParams(vmem_limit_bytes=58 * 2**20),
        cost_estimate=pl.CostEstimate(flops=2 * ops.size * members, bytes_accessed=2 * ops.size, transcendentals=0),
    )(cols, ens_t, left, right, ops)


def gram_kernel(pred_ref, obs_ref, err_ref, out_ref):
    total = out_ref.shape[0]
    half = total // 2
    width = obs_ref.shape[1]
    pred = (pred_ref[:, :, :width].astype(F32) + pred_ref[:, :, width:].astype(F32)).reshape(total, width)
    mean = jnp.sum(pred, axis=0, keepdims=True) / total
    scale = err_ref[...] * math.sqrt(total - 1)
    white = (pred - mean) / scale
    departure = (obs_ref[...] - mean) / scale
    row = lax.broadcasted_iota(jnp.int32, (half, white.shape[1]), 0)
    first = jnp.where(row == 0, departure, 0.0)
    second = jnp.where(row == 1, departure, 0.0)
    top, low = white[:half], white[half:]
    dot = functools.partial(lax.dot_general, dimension_numbers=NT, precision=HIGHEST, preferred_element_type=F32)
    out_ref[:half, :half] = dot(top, top)
    out_ref[:half, half:] = dot(top, first) + dot(low, second)
    out_ref[half:, :] = dot(low, white)


def gram(shared, obs, err):
    sources, members = shared.shape[:2]
    total, width = sources * members, obs.shape[1]
    row = pl.BlockSpec((1, width), lambda i: (0, 0))
    return pl.pallas_call(
        gram_kernel,
        out_shape=jax.ShapeDtypeStruct((total, total), F32),
        grid=(1,),
        in_specs=[pl.BlockSpec((sources, members, 2 * width), lambda i: (0, 0, 0)), row, row],
        out_specs=pl.BlockSpec((total, total), lambda i: (0, 0)),
        compiler_params=pltpu.CompilerParams(vmem_limit_bytes=16 * 2**20),
    )(shared, obs, err)


WIDE = 32


def spread(column):
    return jnp.broadcast_to(column, (8, 128))


def eliminate(panel, col0):
    groups = WIDE // 8
    sub = lax.broadcasted_iota(jnp.int32, (8, 128), 0)
    tile = col0 // 128
    lanes = lax.broadcasted_iota(jnp.int32, (8, 128), 1) + 128 * tile
    tiles = panel[0].shape[1] // 128
    panel = [[p[:, 128 * t : 128 * (t + 1)] for t in range(tiles)] for p in panel]
    out = []
    for q in range(groups):
        start = col0 + 8 * q
        at = start - 128 * tile
        coef = [[None if g < q else spread(panel[g][tile][:, at + c : at + c + 1]) for g in range(groups)] for c in range(8)]
        pivots = jnp.ones((8, 128), F32)
        for j in range(8):
            pivot = spread(coef[j][q][j : j + 1, :])
            pivots = jnp.where(sub == j, pivot, pivots)
            ratio = 1.0 / pivot
            ahead = [spread(coef[c][q][j : j + 1, :]) for c in range(8)]
            for g in range(q, groups):
                times = coef[j][g] * ratio
                if g == q:
                    times = jnp.where(sub > j, times, 0.0)
                for c in range(8):
                    if c == j:
                        coef[c][g] = jnp.where(sub == j, 1.0, -times) if g == q else -times
                    else:
                        coef[c][g] = coef[c][g] - times * ahead[c]
        inside = (lanes >= start) & (lanes < start + 8)
        unit = jnp.where(lanes - start == sub, 1.0, 0.0)
        base = [jnp.where(inside, unit, panel[q][t]) if t == tile else panel[q][t] for t in range(tiles)]
        root = lax.rsqrt(pivots)
        rows = [[spread(base[t][c : c + 1, :]) for t in range(tiles)] for c in range(8)]
        low = [jnp.where(sub >= c, coef[c][q], 0.0) for c in range(8)]
        out.append([sum(low[c] * rows[c][t] for c in range(8)) * root for t in range(tiles)])
        for g in range(q + 1, groups):
            for t in range(tiles):
                here = jnp.where(inside, 0.0, panel[g][t]) if t == tile else panel[g][t]
                panel[g][t] = here + sum(coef[c][g] * rows[c][t] for c in range(8))
    return jnp.concatenate([jnp.concatenate(o, axis=1) for o in out], axis=0)


def transform_kernel(gram_ref, ens_ref, out_ref):
    total = gram_ref.shape[0]
    half = total // 2
    row = lax.broadcasted_iota(jnp.int32, (total, total), 0)
    col = lax.broadcasted_iota(jnp.int32, (total, total), 1)
    given = gram_ref[...]
    extra = given[:half, half:]
    cross = jnp.concatenate([extra[:, 0:1], extra[:, 1:2]], axis=0)
    mirror = given[half:, :half].T
    full = jnp.concatenate([jnp.concatenate([given[:half, :half], mirror], axis=1), given[half:, :]], axis=0)
    full = full + jnp.where(row == col, 1.0, 0.0)
    count = total // WIDE
    blocks = [full[WIDE * t : WIDE * (t + 1), :] for t in range(count)]
    for s in range(count):
        r0, r1 = WIDE * s, WIDE * (s + 1)
        done = eliminate([blocks[s][8 * g : 8 * (g + 1), :] for g in range(WIDE // 8)], r0)
        here = col[r0:r1]
        blocks[s] = jnp.where(here <= row[r0:r1], done, 0.0)
        if r1 < total:
            kept = jnp.where((here < r1) & (here > row[r0:r1]), 0.0, done)
            turned = done.T
            inside = (here >= r0) & (here < r1)
            for t in range(s + 1, count):
                change = jnp.dot(turned[WIDE * t : WIDE * (t + 1), :], kept, precision=HIGHEST, preferred_element_type=F32)
                blocks[t] = jnp.where(inside, 0.0, blocks[t]) - change
    inverse = jnp.concatenate(blocks, axis=0)
    solved = jnp.sum(inverse * cross.T, axis=1, keepdims=True)
    weight = jnp.sum(inverse * solved, axis=0, keepdims=True)
    rounded = (inverse + weight).astype(BF16).astype(F32)
    centred = rounded - jnp.sum(rounded, axis=1, keepdims=True) / total + 1.0 / total
    high = centred.astype(BF16)
    rest = (centred - high.astype(F32)).astype(BF16)
    states = ens_ref[...].reshape(total, -1)
    both = jnp.dot(high, states, preferred_element_type=F32) + jnp.dot(rest, states, preferred_element_type=F32)
    out_ref[...] = both.astype(BF16).reshape(out_ref.shape)


def transform(gram_sum, shared):
    total = gram_sum.shape[0]
    sources, members, width = shared.shape
    block = (sources, members, width // 2)
    return pl.pallas_call(
        transform_kernel,
        out_shape=jax.ShapeDtypeStruct(block, BF16),
        grid=(1,),
        in_specs=[pl.BlockSpec((total, total), lambda i: (0, 0)), pl.BlockSpec(block, lambda i: (0, 0, 1))],
        out_specs=pl.BlockSpec(block, lambda i: (0, 0, 0)),
        compiler_params=pltpu.CompilerParams(vmem_limit_bytes=16 * 2**20),
    )(gram_sum, shared)


def to_all(x, axes, count):
    return lax.all_to_all(jnp.broadcast_to(x[None], (count,) + x.shape), axes, 0, 0, tiled=True)


def local(ensemble, operator_blocks, block_columns, observed, error_scale):
    ens_t = ensemble.T
    members, rows = ens_t.shape
    space_count = lax.axis_size(SPACE)
    member_count = lax.axis_size(MEMBER)
    plane_count = lax.axis_size(PLANE)
    z_count = lax.axis_size("z")
    total = members * member_count
    space_index = lax.axis_index(SPACE)
    member_index = lax.axis_index(MEMBER)
    left = lax.ppermute(ens_t[:, -128:], SPACE, [(i, (i + 1) % space_count) for i in range(space_count)])
    right = lax.ppermute(ens_t[:, :128], SPACE, [((i + 1) % space_count, i) for i in range(space_count)])
    state_local = rows // 128
    cols = jnp.mod(block_columns - space_index * state_local + 1, state_local * space_count)
    shared = predict(cols, ens_t, left, right, operator_blocks, member_count)
    shared = lax.all_to_all(shared, MEMBER, 0, 0, tiled=True)
    count = observed.shape[0] // member_count
    obs = lax.dynamic_slice_in_dim(observed, member_index * count, count)[None]
    err = lax.dynamic_slice_in_dim(error_scale, member_index * count, count)[None]
    part = gram(shared, obs, err).reshape(plane_count, -1, total)
    part = jnp.sum(lax.all_to_all(part, PLANE, 0, 0, tiled=True), axis=0)
    part = jnp.sum(to_all(part, "z", z_count), axis=0)
    gram_sum = to_all(part, PLANE, plane_count).reshape(total, total)
    analysis = lax.all_to_all(transform(gram_sum, shared), MEMBER, 0, 0, tiled=True)
    return analysis.transpose(1, 0, 2).reshape(members, rows).T


def solution(mesh):
    fine = Mesh(mesh.devices.reshape(16, 2, 4, 4), ("z", "core", "y", "x"))
    in_specs = (P(SPACE, MEMBER), P(SPACE, None, None, None), P(SPACE, None), P(SPACE), P(SPACE))
    return jax.shard_map(local, mesh=fine, in_specs=in_specs, out_specs=P(SPACE, MEMBER), check_vma=False)
```

```python
import functools
import math

import jax
import jax.numpy as jnp
from jax import lax
from jax.experimental import pallas as pl
from jax.experimental.pallas import tpu as pltpu
from jax.sharding import Mesh
from jax.sharding import PartitionSpec as P

F32, BF16 = jnp.float32, jnp.bfloat16
HIGHEST = lax.Precision.HIGHEST
NT = (((1,), (1,)), ((), ()))
TN = (((0,), (0,)), ((), ()))
PLANE = ("core", "y", "x")
MEMBER = ("y", "x")
SPACE = ("z", "core")


def predict_kernel(cols_ref, state, left_ref, right_ref, ops_ref, out_ref, weights, staged, sems, out_sems, ens_sems):
    parts = out_ref.shape[0]
    rows = state.shape[1] - 256
    group = ops_ref.shape[0] // parts
    width, share = 128 * group, rows // parts

    def fetch(c):
        return pltpu.make_async_copy(ops_ref.at[pl.ds(c * group, group)], weights.at[pl.ds(c * group, group)], sems.at[c])

    for c in range(4):
        fetch(c).start()
    def deliver(c):
        return pltpu.make_async_copy(staged.at[c], out_ref.at[c, :, pl.ds(0, 2 * width)], out_sems.at[c])

    def pass_on(c):
        chunk = state.at[:, pl.ds(128 + c * share, share)]
        return pltpu.make_async_copy(chunk, out_ref.at[c, :, pl.ds(2 * width, share)], ens_sems.at[c])

    def pick(at):
        inner = state[:, pl.ds(pl.multiple_of(at * 128, 128), 128)]
        return jnp.where(at == 0, left_ref[...], jnp.where(at == rows // 128 + 1, right_ref[...], inner))

    for c in range(parts):
        pass_on(c).start()

    def body(c, carry):
        fetch(c).wait()

        @pl.when(c + 4 < parts)
        def _():
            fetch(c + 4).start()

        for o in range(group):
            block = c * group + o
            picked = [pick(cols_ref[block, k]) for k in range(8)]
            rows_of = [weights[block, k] for k in range(8)]
            value = lax.dot_general(
                jnp.concatenate(picked, axis=1), jnp.concatenate(rows_of, axis=1), NT, preferred_element_type=F32
            )
            high = value.astype(BF16)
            staged[c, :, 128 * o : 128 * (o + 1)] = high
            staged[c, :, width + 128 * o : width + 128 * (o + 1)] = (value - high.astype(F32)).astype(BF16)
        deliver(c).start()
        return carry

    lax.fori_loop(0, parts, body, 0)
    for c in range(parts):
        pass_on(c).wait()
        deliver(c).wait()


def predict(cols, state, left, right, ops, parts):
    members, rows = state.shape[0], state.shape[1] - 256
    oblocks = ops.shape[0]
    outside, inside = pl.BlockSpec(memory_space=pltpu.HBM), pl.BlockSpec(memory_space=pltpu.VMEM)
    return pl.pallas_call(
        predict_kernel,
        out_shape=jax.ShapeDtypeStruct((parts, members, (2 * oblocks * 128 + rows) // parts), BF16),
        in_specs=[pl.BlockSpec(memory_space=pltpu.SMEM), inside, inside, inside, outside],
        out_specs=outside,
        scratch_shapes=[
            pltpu.VMEM(ops.shape, BF16),
            pltpu.VMEM((parts, members, 2 * oblocks * 128 // parts), BF16),
            pltpu.SemaphoreType.DMA((parts,)),
            pltpu.SemaphoreType.DMA((parts,)),
            pltpu.SemaphoreType.DMA((parts,)),
        ],
        compiler_params=pltpu.CompilerParams(vmem_limit_bytes=50 * 2**20),
        cost_estimate=pl.CostEstimate(flops=2 * ops.size * members, bytes_accessed=2 * ops.size, transcendentals=0),
    )(cols, state, left, right, ops)


def gram_kernel(pred_ref, obs_ref, err_ref, out_ref):
    total = out_ref.shape[0]
    half = total // 2
    width = obs_ref.shape[1]
    pred = (pred_ref[:, :, :width].astype(F32) + pred_ref[:, :, width:].astype(F32)).reshape(total, width)
    mean = jnp.sum(pred, axis=0, keepdims=True) / total
    scale = err_ref[...] * math.sqrt(total - 1)
    white = (pred - mean) / scale
    departure = (obs_ref[...] - mean) / scale
    row = lax.broadcasted_iota(jnp.int32, (half, white.shape[1]), 0)
    first = jnp.where(row == 0, departure, 0.0)
    second = jnp.where(row == 1, departure, 0.0)
    top, low = white[:half], white[half:]
    dot = functools.partial(lax.dot_general, dimension_numbers=NT, precision=HIGHEST, preferred_element_type=F32)
    out_ref[:half, :half] = dot(top, top)
    out_ref[:half, half:] = dot(top, first) + dot(low, second)
    out_ref[half:, :] = dot(low, white)


def gram(shared, obs, err):
    sources, members = shared.shape[:2]
    total, width = sources * members, obs.shape[1]
    row = pl.BlockSpec((1, width), lambda i: (0, 0))
    return pl.pallas_call(
        gram_kernel,
        out_shape=jax.ShapeDtypeStruct((total, total), F32),
        grid=(1,),
        in_specs=[pl.BlockSpec((sources, members, 2 * width), lambda i: (0, 0, 0)), row, row],
        out_specs=pl.BlockSpec((total, total), lambda i: (0, 0)),
        compiler_params=pltpu.CompilerParams(vmem_limit_bytes=16 * 2**20),
    )(shared, obs, err)


WIDE = 32
STEP = 16


def spread(column):
    return jnp.broadcast_to(column, (8, 128))


def total_of(terms):
    while len(terms) > 1:
        terms = [a + b for a, b in zip(terms[::2], terms[1::2])] + terms[len(terms) & ~1 :]
    return terms[0]


def eliminate(panel, col0):
    groups, span = WIDE // 8, STEP // 8
    sub = lax.broadcasted_iota(jnp.int32, (8, 128), 0)
    tile = col0 // 128
    lanes = lax.broadcasted_iota(jnp.int32, (8, 128), 1) + 128 * tile
    tiles = panel[0].shape[1] // 128
    order = [tile] + [t for t in range(tiles) if t != tile]
    panel = [[p[:, 128 * t : 128 * (t + 1)] for t in range(tiles)] for p in panel]
    out = []
    for q in range(0, groups, span):
        start = col0 + 8 * q
        at = start - 128 * tile
        coef = [[None if g < q else spread(panel[g][tile][:, at + c : at + c + 1]) for g in range(groups)] for c in range(STEP)]
        pivots = [jnp.ones((8, 128), F32) for _ in range(span)]
        for j in range(STEP):
            own, r = q + j // 8, j % 8
            pivot = spread(coef[j][own][r : r + 1, :])
            pivots[j // 8] = jnp.where(sub == r, pivot, pivots[j // 8])
            ratio = 1.0 / pivot
            ahead = [spread(coef[c][own][r : r + 1, :]) for c in range(STEP)]
            for g in range(own, groups):
                times = coef[j][g] * ratio
                if g == own:
                    times = jnp.where(sub > r, times, 0.0)
                for c in [c for c in range(j + 1, STEP)] + [c for c in range(j + 1)]:
                    if c == j:
                        coef[c][g] = jnp.where(sub == r, 1.0, -times) if g == own else -times
                    else:
                        coef[c][g] = coef[c][g] - times * ahead[c]
        inside = (lanes >= start) & (lanes < start + STEP)
        base = []
        for h in range(span):
            unit = jnp.where(lanes - start == sub + 8 * h, 1.0, 0.0)
            base.append([jnp.where(inside, unit, panel[q + h][t]) if t == tile else panel[q + h][t] for t in range(tiles)])
        rows = [[spread(base[c // 8][t][c % 8 : c % 8 + 1, :]) for t in range(tiles)] for c in range(STEP)]
        for g in range(q + span, groups):
            for t in order:
                here = jnp.where(inside, 0.0, panel[g][t]) if t == tile else panel[g][t]
                panel[g][t] = here + total_of([coef[c][g] * rows[c][t] for c in range(STEP)])
        for h in range(span):
            root = lax.rsqrt(pivots[h])
            low = [jnp.where(sub + 8 * h >= c, coef[c][q + h], 0.0) for c in range(min(STEP, 8 * h + 8))]
            out.append([total_of([low[c] * rows[c][t] for c in range(len(low))]) * root for t in range(tiles)])
    return jnp.concatenate([jnp.concatenate(o, axis=1) for o in out], axis=0)


def transform_kernel(gram_ref, ens_ref, out_ref):
    total = gram_ref.shape[0]
    half = total // 2
    states = ens_ref[...].astype(F32).reshape(total, -1)
    mean_state = jnp.sum(states, axis=0, keepdims=True) / total
    anomalies = (states - mean_state).astype(BF16)
    row = lax.broadcasted_iota(jnp.int32, (total, total), 0)
    col = lax.broadcasted_iota(jnp.int32, (total, total), 1)
    given = gram_ref[...]
    extra = given[:half, half:]
    cross = jnp.concatenate([extra[:, 0:1], extra[:, 1:2]], axis=0).T
    mirror = given[half:, :half].T
    full = jnp.concatenate([jnp.concatenate([given[:half, :half], mirror], axis=1), given[half:, :]], axis=0)
    full = full + jnp.where(row == col, 1.0, 0.0)
    count = total // WIDE
    blocks = [full[WIDE * t : WIDE * (t + 1), :] for t in range(count)]
    weight = jnp.zeros((1, total), F32)
    for s in range(count):
        r0, r1 = WIDE * s, WIDE * (s + 1)
        done = eliminate([blocks[s][8 * g : 8 * (g + 1), :] for g in range(WIDE // 8)], r0)
        here = col[r0:r1]
        blocks[s] = jnp.where(here <= row[r0:r1], done, 0.0)
        if r1 < total:
            kept = jnp.where((here < r1) & (here > row[r0:r1]), 0.0, done)
            turned = done.T
            inside = (here >= r0) & (here < r1)
            for t in range(s + 1, count):
                change = jnp.dot(turned[WIDE * t : WIDE * (t + 1), :], kept, precision=HIGHEST, preferred_element_type=F32)
                blocks[t] = jnp.where(inside, 0.0, blocks[t]) - change
        solved = jnp.sum(blocks[s] * cross, axis=1, keepdims=True)
        weight = weight + jnp.sum(blocks[s] * solved, axis=0, keepdims=True)
    turned = (jnp.concatenate(blocks, axis=0) + weight).astype(BF16)
    change = jnp.dot(turned, anomalies, preferred_element_type=F32)
    out_ref[...] = (mean_state + change).astype(BF16).reshape(out_ref.shape)


def transform(gram_sum, shared):
    total = gram_sum.shape[0]
    sources, members, width = shared.shape
    block = (sources, members, width // 2)
    return pl.pallas_call(
        transform_kernel,
        out_shape=jax.ShapeDtypeStruct(block, BF16),
        grid=(1,),
        in_specs=[pl.BlockSpec((total, total), lambda i: (0, 0)), pl.BlockSpec(block, lambda i: (0, 0, 1))],
        out_specs=pl.BlockSpec(block, lambda i: (0, 0, 0)),
        compiler_params=pltpu.CompilerParams(vmem_limit_bytes=16 * 2**20),
    )(gram_sum, shared)


def to_all(x, axes, count):
    return lax.all_to_all(jnp.broadcast_to(x[None], (count,) + x.shape), axes, 0, 0, tiled=True)


def local(ensemble, operator_blocks, block_columns, observed, error_scale):
    ens_t = ensemble.T
    members, rows = ens_t.shape
    space_count = lax.axis_size(SPACE)
    member_count = lax.axis_size(MEMBER)
    plane_count = lax.axis_size(PLANE)
    z_count = lax.axis_size("z")
    total = members * member_count
    space_index = lax.axis_index(SPACE)
    member_index = lax.axis_index(MEMBER)
    left = lax.ppermute(ens_t[:, -128:], SPACE, [(i, (i + 1) % space_count) for i in range(space_count)])
    right = lax.ppermute(ens_t[:, :128], SPACE, [((i + 1) % space_count, i) for i in range(space_count)])
    state = jnp.pad(ens_t, ((0, 0), (128, 128)))
    state_local = rows // 128
    cols = jnp.mod(block_columns - space_index * state_local + 1, state_local * space_count)
    shared = predict(cols, state, left, right, operator_blocks, member_count)
    shared = lax.all_to_all(shared, MEMBER, 0, 0, tiled=True)
    count = observed.shape[0] // member_count
    obs = lax.dynamic_slice_in_dim(observed, member_index * count, count)[None]
    err = lax.dynamic_slice_in_dim(error_scale, member_index * count, count)[None]
    part = gram(shared, obs, err).reshape(plane_count, -1, total)
    part = jnp.sum(lax.all_to_all(part, PLANE, 0, 0, tiled=True), axis=0)
    part = jnp.sum(to_all(part, "z", z_count), axis=0)
    gram_sum = to_all(part, PLANE, plane_count).reshape(total, total)
    analysis = lax.all_to_all(transform(gram_sum, shared), MEMBER, 0, 0, tiled=True)
    return analysis.transpose(1, 0, 2).reshape(members, rows).T


def solution(mesh):
    fine = Mesh(mesh.devices.reshape(16, 2, 4, 4), ("z", "core", "y", "x"))
    in_specs = (P(SPACE, MEMBER), P(SPACE, None, None, None), P(SPACE, None), P(SPACE), P(SPACE))
    return jax.shard_map(local, mesh=fine, in_specs=in_specs, out_specs=P(SPACE, MEMBER), check_vma=False)
```

```python
import functools
import math

import jax
import jax.numpy as jnp
from jax import lax
from jax.experimental import pallas as pl
from jax.experimental.pallas import tpu as pltpu
from jax.sharding import Mesh
from jax.sharding import PartitionSpec as P

F32, BF16 = jnp.float32, jnp.bfloat16
HIGHEST = lax.Precision.HIGHEST
NT = (((1,), (1,)), ((), ()))
TN = (((0,), (0,)), ((), ()))
PLANE = ("core", "y", "x")
MEMBER = ("y", "x")
SPACE = ("z", "core")


def predict_kernel(cols_ref, state, left_ref, right_ref, ops_ref, out_ref, weights, staged, sems, out_sems, ens_sems):
    parts = out_ref.shape[0]
    rows = state.shape[1] - 256
    group = ops_ref.shape[0] // parts
    width, share = 128 * group, rows // parts

    def fetch(c):
        return pltpu.make_async_copy(ops_ref.at[pl.ds(c * group, group)], weights.at[pl.ds(c * group, group)], sems.at[c])

    for c in range(4):
        fetch(c).start()
    def deliver(c):
        return pltpu.make_async_copy(staged.at[c], out_ref.at[c, :, pl.ds(0, 2 * width)], out_sems.at[c])

    def pass_on(c):
        chunk = state.at[:, pl.ds(128 + c * share, share)]
        return pltpu.make_async_copy(chunk, out_ref.at[c, :, pl.ds(2 * width, share)], ens_sems.at[c])

    def pick(at):
        inner = state[:, pl.ds(pl.multiple_of(at * 128, 128), 128)]
        return jnp.where(at == 0, left_ref[...], jnp.where(at == rows // 128 + 1, right_ref[...], inner))

    for c in range(parts):
        pass_on(c).start()

    def body(c, carry):
        fetch(c).wait()

        @pl.when(c + 4 < parts)
        def _():
            fetch(c + 4).start()

        for o in range(group):
            block = c * group + o
            picked = [pick(cols_ref[block, k]) for k in range(8)]
            rows_of = [weights[block, k] for k in range(8)]
            value = lax.dot_general(
                jnp.concatenate(picked, axis=1), jnp.concatenate(rows_of, axis=1), NT, preferred_element_type=F32
            )
            high = value.astype(BF16)
            staged[c, :, 128 * o : 128 * (o + 1)] = high
            staged[c, :, width + 128 * o : width + 128 * (o + 1)] = (value - high.astype(F32)).astype(BF16)
        deliver(c).start()
        return carry

    lax.fori_loop(0, parts, body, 0)
    for c in range(parts):
        pass_on(c).wait()
        deliver(c).wait()


def predict(cols, state, left, right, ops, parts):
    members, rows = state.shape[0], state.shape[1] - 256
    oblocks = ops.shape[0]
    outside, inside = pl.BlockSpec(memory_space=pltpu.HBM), pl.BlockSpec(memory_space=pltpu.VMEM)
    return pl.pallas_call(
        predict_kernel,
        out_shape=jax.ShapeDtypeStruct((parts, members, (2 * oblocks * 128 + rows) // parts), BF16),
        in_specs=[pl.BlockSpec(memory_space=pltpu.SMEM), inside, inside, inside, outside],
        out_specs=outside,
        scratch_shapes=[
            pltpu.VMEM(ops.shape, BF16),
            pltpu.VMEM((parts, members, 2 * oblocks * 128 // parts), BF16),
            pltpu.SemaphoreType.DMA((parts,)),
            pltpu.SemaphoreType.DMA((parts,)),
            pltpu.SemaphoreType.DMA((parts,)),
        ],
        compiler_params=pltpu.CompilerParams(vmem_limit_bytes=50 * 2**20),
        cost_estimate=pl.CostEstimate(flops=2 * ops.size * members, bytes_accessed=2 * ops.size, transcendentals=0),
    )(cols, state, left, right, ops)


def gram_kernel(pred_ref, obs_ref, err_ref, out_ref):
    total = pred_ref.shape[0] * pred_ref.shape[1]
    half = total // 2
    width = obs_ref.shape[1]
    pred = (pred_ref[:, :, :width].astype(F32) + pred_ref[:, :, width:].astype(F32)).reshape(total, width)
    mean = jnp.sum(pred, axis=0, keepdims=True) / total
    scale = err_ref[...] * math.sqrt(total - 1)
    white = (pred - mean) / scale
    departure = (obs_ref[...] - mean) / scale
    edge = lax.broadcasted_iota(jnp.int32, (8, width), 0)
    top, low = white[:half], white[half:]
    dot = functools.partial(lax.dot_general, dimension_numbers=NT, precision=HIGHEST, preferred_element_type=F32)
    cross = dot(jnp.where(edge == 0, departure, 0.0), white)[:1]
    first, second = dot(top, top), dot(low, low)
    row = lax.broadcasted_iota(jnp.int32, (half, half), 0)
    col = lax.broadcasted_iota(jnp.int32, (half, half), 1)
    diagonal = jnp.sum(jnp.where(row == col, second, 0.0), axis=0, keepdims=True)
    halves = [dot(low, top), jnp.where(row >= col, first, second)]
    extra = [diagonal, cross[:, :half], cross[:, half:]]
    for i in range(out_ref.shape[0]):
        part = halves[8 * i // half]
        for r in range(8):
            at = (8 * i + r) % half
            out_ref[i, :, 128 * r : 128 * (r + 1)] = part[at : at + 1, :]
        out_ref[i, :, 1024:] = extra[i] if i < len(extra) else jnp.zeros((1, 128), F32)


def gram(shared, obs, err):
    sources, members = shared.shape[:2]
    total, width = sources * members, obs.shape[1]
    row = pl.BlockSpec((1, width), lambda i: (0, 0))
    return pl.pallas_call(
        gram_kernel,
        out_shape=jax.ShapeDtypeStruct((total // 8, 1, 1152), F32),
        grid=(1,),
        in_specs=[pl.BlockSpec((sources, members, 2 * width), lambda i: (0, 0, 0)), row, row],
        out_specs=pl.BlockSpec((total // 8, 1, 1152), lambda i: (0, 0, 0)),
        compiler_params=pltpu.CompilerParams(vmem_limit_bytes=16 * 2**20),
    )(shared, obs, err)


WIDE = 32
STEP = 16


def spread(column):
    return jnp.broadcast_to(column, (8, 128))


def total_of(terms):
    while len(terms) > 1:
        terms = [a + b for a, b in zip(terms[::2], terms[1::2])] + terms[len(terms) & ~1 :]
    return terms[0]


def eliminate(panel, col0):
    groups, span = WIDE // 8, STEP // 8
    sub = lax.broadcasted_iota(jnp.int32, (8, 128), 0)
    tile = col0 // 128
    lanes = lax.broadcasted_iota(jnp.int32, (8, 128), 1) + 128 * tile
    tiles = panel[0].shape[1] // 128
    order = [tile] + [t for t in range(tiles) if t != tile]
    panel = [[p[:, 128 * t : 128 * (t + 1)] for t in range(tiles)] for p in panel]
    out = []
    for q in range(0, groups, span):
        start = col0 + 8 * q
        at = start - 128 * tile
        coef = [[None if g < q else spread(panel[g][tile][:, at + c : at + c + 1]) for g in range(groups)] for c in range(STEP)]
        pivots = [jnp.ones((8, 128), F32) for _ in range(span)]
        for j in range(STEP):
            own, r = q + j // 8, j % 8
            pivot = spread(coef[j][own][r : r + 1, :])
            pivots[j // 8] = jnp.where(sub == r, pivot, pivots[j // 8])
            ratio = 1.0 / pivot
            ahead = [spread(coef[c][own][r : r + 1, :]) for c in range(STEP)]
            for g in range(own, groups):
                times = coef[j][g] * ratio
                if g == own:
                    times = jnp.where(sub > r, times, 0.0)
                for c in [c for c in range(j + 1, STEP)] + [c for c in range(j + 1)]:
                    if c == j:
                        coef[c][g] = jnp.where(sub == r, 1.0, -times) if g == own else -times
                    else:
                        coef[c][g] = coef[c][g] - times * ahead[c]
        inside = (lanes >= start) & (lanes < start + STEP)
        base = []
        for h in range(span):
            unit = jnp.where(lanes - start == sub + 8 * h, 1.0, 0.0)
            base.append([jnp.where(inside, unit, panel[q + h][t]) if t == tile else panel[q + h][t] for t in range(tiles)])
        rows = [[spread(base[c // 8][t][c % 8 : c % 8 + 1, :]) for t in range(tiles)] for c in range(STEP)]
        for g in range(q + span, groups):
            for t in order:
                here = jnp.where(inside, 0.0, panel[g][t]) if t == tile else panel[g][t]
                panel[g][t] = here + total_of([coef[c][g] * rows[c][t] for c in range(STEP)])
        for h in range(span):
            root = lax.rsqrt(pivots[h])
            low = [jnp.where(sub + 8 * h >= c, coef[c][q + h], 0.0) for c in range(min(STEP, 8 * h + 8))]
            out.append([total_of([low[c] * rows[c][t] for c in range(len(low))]) * root for t in range(tiles)])
    return jnp.concatenate([jnp.concatenate(o, axis=1) for o in out], axis=0)


def transform_kernel(gram_ref, ens_ref, out_ref, packed):
    total = 8 * gram_ref.shape[0]
    half = total // 2
    states = ens_ref[...].astype(F32).reshape(total, -1)
    mean_state = jnp.sum(states, axis=0, keepdims=True) / total
    anomalies = (states - mean_state).astype(BF16)
    row = lax.broadcasted_iota(jnp.int32, (total, total), 0)
    col = lax.broadcasted_iota(jnp.int32, (total, total), 1)
    for i in range(total // 8):
        for r in range(8):
            packed[8 * i + r : 8 * i + r + 1, :] = gram_ref[i, :, 128 * r : 128 * (r + 1)]
    diagonal, *cross = [gram_ref[i, :, 1024:] for i in range(3)]
    cross = jnp.concatenate(cross, axis=1)
    block, mixed = packed[:half], packed[half:]
    flipped = mixed.T
    above = (row < col)[:half, :half]
    below = (row > col)[:half, :half]
    first = jnp.where(above, flipped, mixed)
    second = jnp.where(above, mixed, jnp.where(below, flipped, diagonal))
    full = jnp.concatenate(
        [jnp.concatenate([first, block.T], axis=1), jnp.concatenate([block, second], axis=1)], axis=0
    )
    full = full + jnp.where(row == col, 1.0, 0.0)
    count = total // WIDE
    blocks = [full[WIDE * t : WIDE * (t + 1), :] for t in range(count)]
    weight = jnp.zeros((1, total), F32)
    for s in range(count):
        r0, r1 = WIDE * s, WIDE * (s + 1)
        done = eliminate([blocks[s][8 * g : 8 * (g + 1), :] for g in range(WIDE // 8)], r0)
        here = col[r0:r1]
        blocks[s] = jnp.where(here <= row[r0:r1], done, 0.0)
        if r1 < total:
            kept = jnp.where((here < r1) & (here > row[r0:r1]), 0.0, done)
            turned = done.T
            inside = (here >= r0) & (here < r1)
            for t in range(s + 1, count):
                change = jnp.dot(turned[WIDE * t : WIDE * (t + 1), :], kept, precision=HIGHEST, preferred_element_type=F32)
                blocks[t] = jnp.where(inside, 0.0, blocks[t]) - change
        solved = jnp.sum(blocks[s] * cross, axis=1, keepdims=True)
        weight = weight + jnp.sum(blocks[s] * solved, axis=0, keepdims=True)
    turned = (jnp.concatenate(blocks, axis=0) + weight).astype(BF16)
    change = jnp.dot(turned, anomalies, preferred_element_type=F32)
    out_ref[...] = (mean_state + change).astype(BF16).reshape(out_ref.shape)


def transform(gram_sum, shared):
    sources, members, width = shared.shape
    block = (sources, members, width // 2)
    return pl.pallas_call(
        transform_kernel,
        out_shape=jax.ShapeDtypeStruct(block, BF16),
        grid=(1,),
        in_specs=[pl.BlockSpec(gram_sum.shape, lambda i: (0, 0, 0)), pl.BlockSpec(block, lambda i: (0, 0, 1))],
        out_specs=pl.BlockSpec(block, lambda i: (0, 0, 0)),
        scratch_shapes=[pltpu.VMEM((sources * members, sources * members // 2), F32)],
        compiler_params=pltpu.CompilerParams(vmem_limit_bytes=16 * 2**20),
    )(gram_sum, shared)


def to_all(x, axes, count):
    return lax.all_to_all(jnp.broadcast_to(x[None], (count,) + x.shape), axes, 0, 0, tiled=True)


def local(ensemble, operator_blocks, block_columns, observed, error_scale):
    ens_t = ensemble.T
    members, rows = ens_t.shape
    space_count = lax.axis_size(SPACE)
    member_count = lax.axis_size(MEMBER)
    plane_count = lax.axis_size(PLANE)
    z_count = lax.axis_size("z")
    total = members * member_count
    space_index = lax.axis_index(SPACE)
    member_index = lax.axis_index(MEMBER)
    left = lax.ppermute(ens_t[:, -128:], SPACE, [(i, (i + 1) % space_count) for i in range(space_count)])
    right = lax.ppermute(ens_t[:, :128], SPACE, [((i + 1) % space_count, i) for i in range(space_count)])
    state = jnp.pad(ens_t, ((0, 0), (128, 128)))
    state_local = rows // 128
    cols = jnp.mod(block_columns - space_index * state_local + 1, state_local * space_count)
    shared = predict(cols, state, left, right, operator_blocks, member_count)
    shared = lax.all_to_all(shared, MEMBER, 0, 0, tiled=True)
    count = observed.shape[0] // member_count
    obs = lax.dynamic_slice_in_dim(observed, member_index * count, count)[None]
    err = lax.dynamic_slice_in_dim(error_scale, member_index * count, count)[None]
    part = gram(shared, obs, err)
    part = jnp.sum(lax.all_to_all(part, PLANE, 0, 0, tiled=True), axis=0)
    part = jnp.sum(to_all(part, "z", z_count), axis=0)
    gram_sum = to_all(part, PLANE, plane_count).reshape(plane_count, 1, -1)
    analysis = lax.all_to_all(transform(gram_sum, shared), MEMBER, 0, 0, tiled=True)
    return analysis.transpose(1, 0, 2).reshape(members, rows).T


def solution(mesh):
    fine = Mesh(mesh.devices.reshape(16, 2, 4, 4), ("z", "core", "y", "x"))
    in_specs = (P(SPACE, MEMBER), P(SPACE, None, None, None), P(SPACE, None), P(SPACE), P(SPACE))
    return jax.shard_map(local, mesh=fine, in_specs=in_specs, out_specs=P(SPACE, MEMBER), check_vma=False)
```

```python
import functools
import math

import jax
import jax.numpy as jnp
from jax import lax
from jax.experimental import pallas as pl
from jax.experimental.pallas import tpu as pltpu
from jax.sharding import Mesh
from jax.sharding import PartitionSpec as P

F32, BF16 = jnp.float32, jnp.bfloat16
HIGHEST = lax.Precision.HIGHEST
NT = (((1,), (1,)), ((), ()))
TN = (((0,), (0,)), ((), ()))
PLANE = ("core", "y", "x")
MEMBER = ("y", "x")
SPACE = ("z", "core")


def predict_kernel(cols_ref, state, left_ref, right_ref, ops_ref, out_ref, weights, staged, sems, out_sems, ens_sems):
    parts = out_ref.shape[0]
    rows = state.shape[1] - 256
    members = state.shape[0]
    group = ops_ref.shape[0] // parts
    sub = lax.broadcasted_iota(jnp.int32, (members, 128), 0)
    width, share = 128 * group, rows // parts

    def fetch(c):
        return pltpu.make_async_copy(ops_ref.at[pl.ds(c * group, group)], weights.at[pl.ds(c * group, group)], sems.at[c])

    for c in range(4):
        fetch(c).start()
    def deliver(c):
        return pltpu.make_async_copy(staged.at[c], out_ref.at[c, :, pl.ds(0, width + 128)], out_sems.at[c])

    def pass_on(c):
        chunk = state.at[:, pl.ds(128 + c * share, share)]
        return pltpu.make_async_copy(chunk, out_ref.at[c, :, pl.ds(width + 128, share)], ens_sems.at[c])

    def pick(at):
        inner = state[:, pl.ds(pl.multiple_of(at * 128, 128), 128)]
        return jnp.where(at == 0, left_ref[...], jnp.where(at == rows // 128 + 1, right_ref[...], inner))

    for c in range(parts):
        pass_on(c).start()

    def body(c, carry):
        fetch(c).wait()

        @pl.when(c + 4 < parts)
        def _():
            fetch(c + 4).start()

        means = jnp.zeros((members, 128), F32)
        for o in range(group):
            block = c * group + o
            picked = [pick(cols_ref[block, k]) for k in range(8)]
            rows_of = [weights[block, k] for k in range(8)]
            value = lax.dot_general(
                jnp.concatenate(picked, axis=1), jnp.concatenate(rows_of, axis=1), NT, preferred_element_type=F32
            )
            mean = jnp.sum(value, axis=0, keepdims=True) / members
            staged[c, :, 128 * o : 128 * (o + 1)] = (value - mean).astype(BF16)
            for part in range(3):
                taken = mean.astype(BF16).astype(F32)
                means = jnp.where(sub == group * part + o, taken, means)
                mean = mean - taken
        staged[c, :, width:] = means.astype(BF16)
        deliver(c).start()
        return carry

    lax.fori_loop(0, parts, body, 0)
    for c in range(parts):
        pass_on(c).wait()
        deliver(c).wait()


def predict(cols, state, left, right, ops, parts):
    members, rows = state.shape[0], state.shape[1] - 256
    oblocks = ops.shape[0]
    outside, inside = pl.BlockSpec(memory_space=pltpu.HBM), pl.BlockSpec(memory_space=pltpu.VMEM)
    return pl.pallas_call(
        predict_kernel,
        out_shape=jax.ShapeDtypeStruct((parts, members, (oblocks * 128 + rows) // parts + 128), BF16),
        in_specs=[pl.BlockSpec(memory_space=pltpu.SMEM), inside, inside, inside, outside],
        out_specs=outside,
        scratch_shapes=[
            pltpu.VMEM(ops.shape, BF16),
            pltpu.VMEM((parts, members, oblocks * 128 // parts + 128), BF16),
            pltpu.SemaphoreType.DMA((parts,)),
            pltpu.SemaphoreType.DMA((parts,)),
            pltpu.SemaphoreType.DMA((parts,)),
        ],
        compiler_params=pltpu.CompilerParams(vmem_limit_bytes=50 * 2**20),
        cost_estimate=pl.CostEstimate(flops=2 * ops.size * members, bytes_accessed=2 * ops.size, transcendentals=0),
    )(cols, state, left, right, ops)


def gram_kernel(pred_ref, obs_ref, err_ref, out_ref):
    total = pred_ref.shape[0] * pred_ref.shape[1]
    half = total // 2
    width = obs_ref.shape[1]
    parts = pred_ref[:, :, width : width + 128].astype(F32)
    group = width // 128
    means = parts[:, :group] + parts[:, group : 2 * group] + parts[:, 2 * group : 3 * group]
    means = jnp.concatenate([means[:, o : o + 1] for o in range(group)], axis=2)
    pred = (pred_ref[:, :, :width].astype(F32) + means).reshape(total, width)
    mean = jnp.sum(pred, axis=0, keepdims=True) / total
    scale = err_ref[...] * math.sqrt(total - 1)
    white = (pred - mean) / scale
    departure = (obs_ref[...] - mean) / scale
    edge = lax.broadcasted_iota(jnp.int32, (8, width), 0)
    top, low = white[:half], white[half:]
    dot = functools.partial(lax.dot_general, dimension_numbers=NT, precision=HIGHEST, preferred_element_type=F32)
    cross = dot(jnp.where(edge == 0, departure, 0.0), white)[:1]
    first, second = dot(top, top), dot(low, low)
    row = lax.broadcasted_iota(jnp.int32, (half, half), 0)
    col = lax.broadcasted_iota(jnp.int32, (half, half), 1)
    diagonal = jnp.sum(jnp.where(row == col, second, 0.0), axis=0, keepdims=True)
    halves = [dot(low, top), jnp.where(row >= col, first, second)]
    extra = [diagonal, cross[:, :half], cross[:, half:]]
    for i in range(out_ref.shape[0]):
        part = halves[8 * i // half]
        for r in range(8):
            at = (8 * i + r) % half
            out_ref[i, :, 128 * r : 128 * (r + 1)] = part[at : at + 1, :]
        out_ref[i, :, 1024:] = extra[i] if i < len(extra) else jnp.zeros((1, 128), F32)


def gram(shared, obs, err):
    total = shared.shape[0] * shared.shape[1]
    return pl.pallas_call(
        gram_kernel,
        out_shape=jax.ShapeDtypeStruct((total // 8, 1, 1152), F32),
        compiler_params=pltpu.CompilerParams(vmem_limit_bytes=16 * 2**20),
    )(shared, obs, err)


WIDE = 32
STEP = 16


def spread(column):
    return jnp.broadcast_to(column, (8, 128))


def total_of(terms):
    while len(terms) > 1:
        terms = [a + b for a, b in zip(terms[::2], terms[1::2])] + terms[len(terms) & ~1 :]
    return terms[0]


def eliminate(panel, col0):
    groups, span = WIDE // 8, STEP // 8
    sub = lax.broadcasted_iota(jnp.int32, (8, 128), 0)
    tile = col0 // 128
    lanes = lax.broadcasted_iota(jnp.int32, (8, 128), 1) + 128 * tile
    tiles = panel[0].shape[1] // 128
    order = [tile] + [t for t in range(tiles) if t != tile]
    panel = [[p[:, 128 * t : 128 * (t + 1)] for t in range(tiles)] for p in panel]
    out = []
    for q in range(0, groups, span):
        start = col0 + 8 * q
        at = start - 128 * tile
        coef = [[None if g < q else spread(panel[g][tile][:, at + c : at + c + 1]) for g in range(groups)] for c in range(STEP)]
        pivots = [jnp.ones((8, 128), F32) for _ in range(span)]
        for j in range(STEP):
            own, r = q + j // 8, j % 8
            pivot = spread(coef[j][own][r : r + 1, :])
            pivots[j // 8] = jnp.where(sub == r, pivot, pivots[j // 8])
            ratio = 1.0 / pivot
            ahead = [spread(coef[c][own][r : r + 1, :]) for c in range(STEP)]
            for g in range(own, groups):
                times = coef[j][g] * ratio
                if g == own:
                    times = jnp.where(sub > r, times, 0.0)
                for c in [c for c in range(j + 1, STEP)] + [c for c in range(j + 1)]:
                    if c == j:
                        coef[c][g] = jnp.where(sub == r, 1.0, -times) if g == own else -times
                    else:
                        coef[c][g] = coef[c][g] - times * ahead[c]
        inside = (lanes >= start) & (lanes < start + STEP)
        base = []
        for h in range(span):
            unit = jnp.where(lanes - start == sub + 8 * h, 1.0, 0.0)
            base.append([jnp.where(inside, unit, panel[q + h][t]) if t == tile else panel[q + h][t] for t in range(tiles)])
        rows = [[spread(base[c // 8][t][c % 8 : c % 8 + 1, :]) for t in range(tiles)] for c in range(STEP)]
        for g in range(q + span, groups):
            for t in order:
                here = jnp.where(inside, 0.0, panel[g][t]) if t == tile else panel[g][t]
                panel[g][t] = here + total_of([coef[c][g] * rows[c][t] for c in range(STEP)])
        for h in range(span):
            root = lax.rsqrt(pivots[h])
            low = [jnp.where(sub + 8 * h >= c, coef[c][q + h], 0.0) for c in range(min(STEP, 8 * h + 8))]
            out.append([total_of([low[c] * rows[c][t] for c in range(len(low))]) * root for t in range(tiles)])
    return jnp.concatenate([jnp.concatenate(o, axis=1) for o in out], axis=0)


def transform_kernel(gram_ref, ens_ref, out_ref, packed):
    total = 8 * gram_ref.shape[0]
    half = total // 2
    states = ens_ref[:, :, ens_ref.shape[2] - out_ref.shape[2] :].astype(F32).reshape(total, -1)
    mean_state = jnp.sum(states, axis=0, keepdims=True) / total
    anomalies = (states - mean_state).astype(BF16)
    row = lax.broadcasted_iota(jnp.int32, (total, total), 0)
    col = lax.broadcasted_iota(jnp.int32, (total, total), 1)
    for i in range(total // 8):
        for r in range(8):
            packed[8 * i + r : 8 * i + r + 1, :] = gram_ref[i, :, 128 * r : 128 * (r + 1)]
    diagonal, *cross = [gram_ref[i, :, 1024:] for i in range(3)]
    cross = jnp.concatenate(cross, axis=1)
    block, mixed = packed[:half], packed[half:]
    flipped = mixed.T
    above = (row < col)[:half, :half]
    below = (row > col)[:half, :half]
    first = jnp.where(above, flipped, mixed)
    second = jnp.where(above, mixed, jnp.where(below, flipped, diagonal))
    full = jnp.concatenate(
        [jnp.concatenate([first, block.T], axis=1), jnp.concatenate([block, second], axis=1)], axis=0
    )
    full = full + jnp.where(row == col, 1.0, 0.0)
    count = total // WIDE
    blocks = [full[WIDE * t : WIDE * (t + 1), :] for t in range(count)]
    weight = jnp.zeros((1, total), F32)
    for s in range(count):
        r0, r1 = WIDE * s, WIDE * (s + 1)
        done = eliminate([blocks[s][8 * g : 8 * (g + 1), :] for g in range(WIDE // 8)], r0)
        here = col[r0:r1]
        blocks[s] = jnp.where(here <= row[r0:r1], done, 0.0)
        if r1 < total:
            kept = jnp.where((here < r1) & (here > row[r0:r1]), 0.0, done)
            turned = done.T
            inside = (here >= r0) & (here < r1)
            for t in range(s + 1, count):
                change = jnp.dot(turned[WIDE * t : WIDE * (t + 1), :], kept, precision=HIGHEST, preferred_element_type=F32)
                blocks[t] = jnp.where(inside, 0.0, blocks[t]) - change
        solved = jnp.sum(blocks[s] * cross, axis=1, keepdims=True)
        weight = weight + jnp.sum(blocks[s] * solved, axis=0, keepdims=True)
    turned = (jnp.concatenate(blocks, axis=0) + weight).astype(BF16)
    change = jnp.dot(turned, anomalies, preferred_element_type=F32)
    out_ref[...] = (mean_state + change).astype(BF16).reshape(out_ref.shape)


def transform(gram_sum, shared, width):
    sources, members = shared.shape[:2]
    return pl.pallas_call(
        transform_kernel,
        out_shape=jax.ShapeDtypeStruct((sources, members, width), BF16),
        scratch_shapes=[pltpu.VMEM((sources * members, sources * members // 2), F32)],
        compiler_params=pltpu.CompilerParams(vmem_limit_bytes=16 * 2**20),
    )(gram_sum, shared)


def to_all(x, axes, count):
    return lax.all_to_all(jnp.broadcast_to(x[None], (count,) + x.shape), axes, 0, 0, tiled=True)


def local(ensemble, operator_blocks, block_columns, observed, error_scale):
    ens_t = ensemble.T
    members, rows = ens_t.shape
    space_count = lax.axis_size(SPACE)
    member_count = lax.axis_size(MEMBER)
    plane_count = lax.axis_size(PLANE)
    z_count = lax.axis_size("z")
    total = members * member_count
    space_index = lax.axis_index(SPACE)
    member_index = lax.axis_index(MEMBER)
    left = lax.ppermute(ens_t[:, -128:], SPACE, [(i, (i + 1) % space_count) for i in range(space_count)])
    right = lax.ppermute(ens_t[:, :128], SPACE, [((i + 1) % space_count, i) for i in range(space_count)])
    state = jnp.pad(ens_t, ((0, 0), (128, 128)))
    state_local = rows // 128
    cols = jnp.mod(block_columns - space_index * state_local + 1, state_local * space_count)
    shared = predict(cols, state, left, right, operator_blocks, member_count)
    shared = lax.all_to_all(shared, MEMBER, 0, 0, tiled=True)
    count = observed.shape[0] // member_count
    obs = lax.dynamic_slice_in_dim(observed, member_index * count, count)[None]
    err = lax.dynamic_slice_in_dim(error_scale, member_index * count, count)[None]
    part = gram(shared, obs, err)
    part = jnp.sum(lax.all_to_all(part, PLANE, 0, 0, tiled=True), axis=0)
    part = jnp.sum(to_all(part, "z", z_count), axis=0)
    gram_sum = to_all(part, PLANE, plane_count).reshape(plane_count, 1, -1)
    analysis = lax.all_to_all(transform(gram_sum, shared, rows // member_count), MEMBER, 0, 0, tiled=True)
    return analysis.transpose(1, 0, 2).reshape(members, rows).T


def solution(mesh):
    fine = Mesh(mesh.devices.reshape(16, 2, 4, 4), ("z", "core", "y", "x"))
    in_specs = (P(SPACE, MEMBER), P(SPACE, None, None, None), P(SPACE, None), P(SPACE), P(SPACE))
    return jax.shard_map(local, mesh=fine, in_specs=in_specs, out_specs=P(SPACE, MEMBER), check_vma=False)
```

```python
import functools
import math

import jax
import jax.numpy as jnp
from jax import lax
from jax.experimental import pallas as pl
from jax.experimental.pallas import tpu as pltpu
from jax.sharding import Mesh
from jax.sharding import PartitionSpec as P

F32, BF16 = jnp.float32, jnp.bfloat16
HIGHEST = lax.Precision.HIGHEST
NT = (((1,), (1,)), ((), ()))
TN = (((0,), (0,)), ((), ()))
PLANE = ("core", "y", "x")
MEMBER = ("y", "x")
SPACE = ("z", "core")


def predict_kernel(
    cols_ref, state, left_ref, right_ref, scaled_ref, inverse_ref, ops_ref, out_ref, lost_ref, weights, raw, staged, sems, out_sems, ens_sems
):
    parts = out_ref.shape[0]
    rows = state.shape[1] - 256
    members = state.shape[0]
    group = ops_ref.shape[0] // parts
    sub = lax.broadcasted_iota(jnp.int32, (members, 128), 0)
    width, share = 128 * group, rows // parts

    def fetch(c):
        return pltpu.make_async_copy(ops_ref.at[pl.ds(c * group, group)], weights.at[pl.ds(c * group, group)], sems.at[c])

    for c in range(4):
        fetch(c).start()
    def deliver(c):
        return pltpu.make_async_copy(staged.at[c], out_ref.at[c, :, pl.ds(0, width + 128)], out_sems.at[c])

    def pass_on(c):
        chunk = state.at[:, pl.ds(pl.multiple_of(128 + c * share, 128), share)]
        return pltpu.make_async_copy(chunk, out_ref.at[c, :, pl.ds(width + 128, share)], ens_sems.at[c])

    def pick(at):
        inner = state[:, pl.ds(pl.multiple_of(at * 128, 128), 128)]
        return jnp.where(at == 0, left_ref[...], jnp.where(at == rows // 128 + 1, right_ref[...], inner))


    def multiply(c):
        values = []
        for o in range(group):
            block = c * group + o
            picked = [pick(cols_ref[block, k]) for k in range(8)]
            rows_of = [weights[block, k] for k in range(8)]
            values.append(
                lax.dot_general(
                    jnp.concatenate(picked, axis=1), jnp.concatenate(rows_of, axis=1), NT, preferred_element_type=F32
                )
            )
        raw[lax.rem(c, 2)] = jnp.concatenate(values, axis=1)

    def split(c, values, lost):
        means = jnp.zeros((members, 128), F32)
        for o in range(group):
            block = c * group + o
            value = values[:, 128 * o : 128 * (o + 1)]
            mean = jnp.sum(value, axis=0, keepdims=True) / members
            rounded = (value - mean).astype(BF16)
            staged[c, :, 128 * o : 128 * (o + 1)] = rounded
            inverse = inverse_ref[pl.ds(block, 1), :]
            departure = scaled_ref[pl.ds(block, 1), :] - mean * inverse
            lost = lost + (value - mean - rounded.astype(F32)) * inverse * departure
            for part in range(3):
                taken = mean.astype(BF16).astype(F32)
                means = jnp.where(sub == group * part + o, taken, means)
                mean = mean - taken
        staged[c, :, width:] = means.astype(BF16)
        deliver(c).start()
        pass_on(c).start()
        return lost

    def body(c, lost):
        fetch(c).wait()

        @pl.when(c + 4 < parts)
        def _():
            fetch(c + 4).start()

        values = raw[lax.rem(c - 1, 2)]
        multiply(c)
        return split(c - 1, values, lost)

    fetch(0).wait()
    fetch(4).start()
    multiply(0)
    lost = lax.fori_loop(1, parts, body, jnp.zeros((members, 128), F32))
    lost_ref[...] = split(parts - 1, raw[(parts - 1) % 2], lost)
    for c in range(parts):
        pass_on(c).wait()
        deliver(c).wait()


def predict(cols, state, left, right, scaled, inverse, ops, parts):
    members, rows = state.shape[0], state.shape[1] - 256
    oblocks = ops.shape[0]
    outside, inside = pl.BlockSpec(memory_space=pltpu.HBM), pl.BlockSpec(memory_space=pltpu.VMEM)
    return pl.pallas_call(
        predict_kernel,
        out_shape=[
            jax.ShapeDtypeStruct((parts, members, (oblocks * 128 + rows) // parts + 128), BF16),
            jax.ShapeDtypeStruct((members, 128), F32),
        ],
        in_specs=[pl.BlockSpec(memory_space=pltpu.SMEM)] + [inside] * 5 + [outside],
        out_specs=[outside, inside],
        scratch_shapes=[
            pltpu.VMEM(ops.shape, BF16),
            pltpu.VMEM((2, members, oblocks * 128 // parts), F32),
            pltpu.VMEM((parts, members, oblocks * 128 // parts + 128), BF16),
            pltpu.SemaphoreType.DMA((parts,)),
            pltpu.SemaphoreType.DMA((parts,)),
            pltpu.SemaphoreType.DMA((parts,)),
        ],
        compiler_params=pltpu.CompilerParams(vmem_limit_bytes=50 * 2**20),
        cost_estimate=pl.CostEstimate(flops=2 * ops.size * members, bytes_accessed=2 * ops.size, transcendentals=0),
    )(cols, state, left, right, scaled, inverse, ops)


def gram_kernel(mine_ref, lost_ref, pred_ref, obs_ref, err_ref, out_ref):
    total = pred_ref.shape[0] * pred_ref.shape[1]
    half = total // 2
    width = obs_ref.shape[1]
    parts = pred_ref[:, :, width : width + 128].astype(F32)
    group = width // 128
    means = parts[:, :group] + parts[:, group : 2 * group] + parts[:, 2 * group : 3 * group]
    means = jnp.concatenate([means[:, o : o + 1] for o in range(group)], axis=2)
    pred = (pred_ref[:, :, :width].astype(F32) + means).reshape(total, width)
    mean = jnp.sum(pred, axis=0, keepdims=True) / total
    scale = err_ref[...] * math.sqrt(total - 1)
    white = (pred - mean) / scale
    departure = (obs_ref[...] - mean) / scale
    edge = lax.broadcasted_iota(jnp.int32, (8, width), 0)
    top, low = white[:half], white[half:]
    dot = functools.partial(lax.dot_general, dimension_numbers=NT, precision=HIGHEST, preferred_element_type=F32)
    cross = dot(jnp.where(edge == 0, departure, 0.0), white)[:1]
    members = lost_ref.shape[0]
    member = lax.broadcasted_iota(jnp.int32, (members, total), 0) + mine_ref[0] * members
    own = member == lax.broadcasted_iota(jnp.int32, (members, total), 1)
    lost = jnp.sum(lost_ref[...], axis=1, keepdims=True)
    cross = cross + jnp.sum(jnp.where(own, lost, 0.0), axis=0, keepdims=True)
    first, second = dot(top, top), dot(low, low)
    row = lax.broadcasted_iota(jnp.int32, (half, half), 0)
    col = lax.broadcasted_iota(jnp.int32, (half, half), 1)
    diagonal = jnp.sum(jnp.where(row == col, second, 0.0), axis=0, keepdims=True)
    halves = [dot(low, top), jnp.where(row >= col, first, second)]
    extra = [diagonal, cross[:, :half], cross[:, half:]]
    for i in range(out_ref.shape[0]):
        part = halves[8 * i // half]
        for r in range(8):
            at = (8 * i + r) % half
            out_ref[i, :, 128 * r : 128 * (r + 1)] = part[at : at + 1, :]
        out_ref[i, :, 1024:] = extra[i] if i < len(extra) else jnp.zeros((1, 128), F32)


def gram(mine, lost, shared, obs, err):
    total = shared.shape[0] * shared.shape[1]
    return pl.pallas_call(
        gram_kernel,
        out_shape=jax.ShapeDtypeStruct((total // 8, 1, 1152), F32),
        in_specs=[pl.BlockSpec(memory_space=pltpu.SMEM)] + [pl.BlockSpec(memory_space=pltpu.VMEM)] * 4,
        compiler_params=pltpu.CompilerParams(vmem_limit_bytes=16 * 2**20),
    )(mine, lost, shared, obs, err)


WIDE = 32
STEP = 16


def spread(column):
    return jnp.broadcast_to(column, (8, 128))


def total_of(terms):
    while len(terms) > 1:
        terms = [a + b for a, b in zip(terms[::2], terms[1::2])] + terms[len(terms) & ~1 :]
    return terms[0]


def eliminate(panel, col0):
    groups, span = WIDE // 8, STEP // 8
    sub = lax.broadcasted_iota(jnp.int32, (8, 128), 0)
    tile = col0 // 128
    lanes = lax.broadcasted_iota(jnp.int32, (8, 128), 1) + 128 * tile
    tiles = panel[0].shape[1] // 128
    order = [tile] + [t for t in range(tiles) if t != tile]
    panel = [[p[:, 128 * t : 128 * (t + 1)] for t in range(tiles)] for p in panel]
    out = []
    for q in range(0, groups, span):
        start = col0 + 8 * q
        at = start - 128 * tile
        coef = [[None if g < q else spread(panel[g][tile][:, at + c : at + c + 1]) for g in range(groups)] for c in range(STEP)]
        pivots = [jnp.ones((8, 128), F32) for _ in range(span)]
        for j in range(STEP):
            own, r = q + j // 8, j % 8
            pivot = spread(coef[j][own][r : r + 1, :])
            pivots[j // 8] = jnp.where(sub == r, pivot, pivots[j // 8])
            ratio = 1.0 / pivot
            ahead = [spread(coef[c][own][r : r + 1, :]) for c in range(STEP)]
            for g in range(own, groups):
                times = coef[j][g] * ratio
                if g == own:
                    times = jnp.where(sub > r, times, 0.0)
                for c in [c for c in range(j + 1, STEP)] + [c for c in range(j + 1)]:
                    if c == j:
                        coef[c][g] = jnp.where(sub == r, 1.0, -times) if g == own else -times
                    else:
                        coef[c][g] = coef[c][g] - times * ahead[c]
        inside = (lanes >= start) & (lanes < start + STEP)
        base = []
        for h in range(span):
            unit = jnp.where(lanes - start == sub + 8 * h, 1.0, 0.0)
            base.append([jnp.where(inside, unit, panel[q + h][t]) if t == tile else panel[q + h][t] for t in range(tiles)])
        rows = [[spread(base[c // 8][t][c % 8 : c % 8 + 1, :]) for t in range(tiles)] for c in range(STEP)]
        for g in range(q + span, groups):
            for t in order:
                here = jnp.where(inside, 0.0, panel[g][t]) if t == tile else panel[g][t]
                panel[g][t] = here + total_of([coef[c][g] * rows[c][t] for c in range(STEP)])
        for h in range(span):
            root = lax.rsqrt(pivots[h])
            low = [jnp.where(sub + 8 * h >= c, coef[c][q + h], 0.0) for c in range(min(STEP, 8 * h + 8))]
            out.append([total_of([low[c] * rows[c][t] for c in range(len(low))]) * root for t in range(tiles)])
    return jnp.concatenate([jnp.concatenate(o, axis=1) for o in out], axis=0)


def transform_kernel(gram_ref, ens_ref, out_ref, packed):
    total = 8 * gram_ref.shape[0]
    half = total // 2
    states = ens_ref[:, :, ens_ref.shape[2] - out_ref.shape[2] :].astype(F32).reshape(total, -1)
    mean_state = jnp.sum(states, axis=0, keepdims=True) / total
    anomalies = (states - mean_state).astype(BF16)
    row = lax.broadcasted_iota(jnp.int32, (total, total), 0)
    col = lax.broadcasted_iota(jnp.int32, (total, total), 1)
    for i in range(total // 8):
        for r in range(8):
            packed[8 * i + r : 8 * i + r + 1, :] = gram_ref[i, :, 128 * r : 128 * (r + 1)]
    diagonal, *cross = [gram_ref[i, :, 1024:] for i in range(3)]
    cross = jnp.concatenate(cross, axis=1)
    block, mixed = packed[:half], packed[half:]
    flipped = mixed.T
    above = (row < col)[:half, :half]
    below = (row > col)[:half, :half]
    first = jnp.where(above, flipped, mixed)
    second = jnp.where(above, mixed, jnp.where(below, flipped, diagonal))
    full = jnp.concatenate(
        [jnp.concatenate([first, block.T], axis=1), jnp.concatenate([block, second], axis=1)], axis=0
    )
    full = full + jnp.where(row == col, 1.0, 0.0)
    count = total // WIDE
    blocks = [full[WIDE * t : WIDE * (t + 1), :] for t in range(count)]
    weight = jnp.zeros((1, total), F32)
    for s in range(count):
        r0, r1 = WIDE * s, WIDE * (s + 1)
        done = eliminate([blocks[s][8 * g : 8 * (g + 1), :] for g in range(WIDE // 8)], r0)
        here = col[r0:r1]
        blocks[s] = jnp.where(here <= row[r0:r1], done, 0.0)
        if r1 < total:
            kept = jnp.where((here < r1) & (here > row[r0:r1]), 0.0, done)
            turned = done.T
            inside = (here >= r0) & (here < r1)
            for t in range(s + 1, count):
                change = jnp.dot(turned[WIDE * t : WIDE * (t + 1), :], kept, precision=HIGHEST, preferred_element_type=F32)
                blocks[t] = jnp.where(inside, 0.0, blocks[t]) - change
        solved = jnp.sum(blocks[s] * cross, axis=1, keepdims=True)
        weight = weight + jnp.sum(blocks[s] * solved, axis=0, keepdims=True)
    turned = (jnp.concatenate(blocks, axis=0) + weight).astype(BF16)
    change = jnp.dot(turned, anomalies, preferred_element_type=F32)
    out_ref[...] = (mean_state + change).astype(BF16).reshape(out_ref.shape)


def transform(gram_sum, shared, width):
    sources, members = shared.shape[:2]
    return pl.pallas_call(
        transform_kernel,
        out_shape=jax.ShapeDtypeStruct((sources, members, width), BF16),
        scratch_shapes=[pltpu.VMEM((sources * members, sources * members // 2), F32)],
        compiler_params=pltpu.CompilerParams(vmem_limit_bytes=16 * 2**20),
    )(gram_sum, shared)


def to_all(x, axes, count):
    return lax.all_to_all(jnp.broadcast_to(x[None], (count,) + x.shape), axes, 0, 0, tiled=True)


def local(ensemble, operator_blocks, block_columns, observed, error_scale):
    ens_t = ensemble.T
    members, rows = ens_t.shape
    space_count = lax.axis_size(SPACE)
    member_count = lax.axis_size(MEMBER)
    plane_count = lax.axis_size(PLANE)
    z_count = lax.axis_size("z")
    total = members * member_count
    space_index = lax.axis_index(SPACE)
    member_index = lax.axis_index(MEMBER)
    left = lax.ppermute(ens_t[:, -128:], SPACE, [(i, (i + 1) % space_count) for i in range(space_count)])
    right = lax.ppermute(ens_t[:, :128], SPACE, [((i + 1) % space_count, i) for i in range(space_count)])
    state = jnp.pad(ens_t, ((0, 0), (128, 128)))
    state_local = rows // 128
    cols = jnp.mod(block_columns - space_index * state_local + 1, state_local * space_count)
    inverse = 1.0 / (error_scale * math.sqrt(total - 1))
    scaled = (observed * inverse).reshape(-1, 128)
    shared, lost = predict(cols, state, left, right, scaled, inverse.reshape(-1, 128), operator_blocks, member_count)
    shared = lax.all_to_all(shared, MEMBER, 0, 0, tiled=True)
    count = observed.shape[0] // member_count
    obs = lax.dynamic_slice_in_dim(observed, member_index * count, count)[None]
    err = lax.dynamic_slice_in_dim(error_scale, member_index * count, count)[None]
    part = gram(member_index.astype(jnp.int32).reshape(1), lost, shared, obs, err)
    part = jnp.sum(lax.all_to_all(part, PLANE, 0, 0, tiled=True), axis=0)
    part = jnp.sum(to_all(part, "z", z_count), axis=0)
    gram_sum = to_all(part, PLANE, plane_count).reshape(plane_count, 1, -1)
    analysis = lax.all_to_all(transform(gram_sum, shared, rows // member_count), MEMBER, 0, 0, tiled=True)
    return analysis.transpose(1, 0, 2).reshape(members, rows).T


def solution(mesh):
    fine = Mesh(mesh.devices.reshape(16, 2, 4, 4), ("z", "core", "y", "x"))
    in_specs = (P(SPACE, MEMBER), P(SPACE, None, None, None), P(SPACE, None), P(SPACE), P(SPACE))
    return jax.shard_map(local, mesh=fine, in_specs=in_specs, out_specs=P(SPACE, MEMBER), check_vma=False)
```

```python
import functools
import math

import jax
import jax.numpy as jnp
from jax import lax
from jax.experimental import pallas as pl
from jax.experimental.pallas import tpu as pltpu
from jax.sharding import Mesh
from jax.sharding import PartitionSpec as P

F32, BF16 = jnp.float32, jnp.bfloat16
HIGHEST = lax.Precision.HIGHEST
NT = (((1,), (1,)), ((), ()))
TN = (((0,), (0,)), ((), ()))
PLANE = ("core", "y", "x")
MEMBER = ("y", "x")
SPACE = ("z", "core")
EXCHANGE = ("x", "y")


def turned(count):
    side = math.isqrt(count)
    return [i % side * side + i // side for i in range(count)]


def predict_kernel(
    cols_ref, state, left_ref, right_ref, scaled_ref, inverse_ref, ops_ref, out_ref, lost_ref, weights, raw, staged, sems, out_sems, ens_sems
):
    parts = out_ref.shape[0]
    rows = state.shape[1] - 256
    members = state.shape[0]
    group = ops_ref.shape[0] // parts
    sub = lax.broadcasted_iota(jnp.int32, (members, 128), 0)
    width, share = 128 * group, rows // parts

    def fetch(c):
        return pltpu.make_async_copy(ops_ref.at[pl.ds(c * group, group)], weights.at[pl.ds(c * group, group)], sems.at[c])

    for c in range(4):
        fetch(c).start()
    def deliver(c):
        return pltpu.make_async_copy(staged.at[c], out_ref.at[c, :, pl.ds(0, width + 128)], out_sems.at[c])

    def pass_on(c):
        chunk = state.at[:, pl.ds(pl.multiple_of(128 + c * share, 128), share)]
        return pltpu.make_async_copy(chunk, out_ref.at[c, :, pl.ds(width + 128, share)], ens_sems.at[c])

    def pick(at):
        inner = state[:, pl.ds(pl.multiple_of(at * 128, 128), 128)]
        return jnp.where(at == 0, left_ref[...], jnp.where(at == rows // 128 + 1, right_ref[...], inner))


    def multiply(c):
        values = []
        for o in range(group):
            block = c * group + o
            picked = [pick(cols_ref[block, k]) for k in range(8)]
            rows_of = [weights[block, k] for k in range(8)]
            values.append(
                lax.dot_general(
                    jnp.concatenate(picked, axis=1), jnp.concatenate(rows_of, axis=1), NT, preferred_element_type=F32
                )
            )
        raw[lax.rem(c, 2)] = jnp.concatenate(values, axis=1)

    def split(c, values, lost):
        means = jnp.zeros((members, 128), F32)
        for o in range(group):
            block = c * group + o
            value = values[:, 128 * o : 128 * (o + 1)]
            mean = jnp.sum(value, axis=0, keepdims=True) / members
            rounded = (value - mean).astype(BF16)
            staged[c, :, 128 * o : 128 * (o + 1)] = rounded
            inverse = inverse_ref[pl.ds(block, 1), :]
            departure = scaled_ref[pl.ds(block, 1), :] - mean * inverse
            lost = lost + (value - mean - rounded.astype(F32)) * inverse * departure
            for part in range(3):
                taken = mean.astype(BF16).astype(F32)
                means = jnp.where(sub == group * part + o, taken, means)
                mean = mean - taken
        staged[c, :, width:] = means.astype(BF16)
        deliver(c).start()
        pass_on(c).start()
        return lost

    def body(c, lost):
        fetch(c).wait()

        @pl.when(c + 4 < parts)
        def _():
            fetch(c + 4).start()

        values = raw[lax.rem(c - 1, 2)]
        multiply(c)
        return split(c - 1, values, lost)

    fetch(0).wait()
    fetch(4).start()
    multiply(0)
    lost = lax.fori_loop(1, parts, body, jnp.zeros((members, 128), F32))
    lost_ref[...] = split(parts - 1, raw[(parts - 1) % 2], lost)
    for c in range(parts):
        pass_on(c).wait()
        deliver(c).wait()


def predict(cols, state, left, right, scaled, inverse, ops, parts):
    members, rows = state.shape[0], state.shape[1] - 256
    oblocks = ops.shape[0]
    outside, inside = pl.BlockSpec(memory_space=pltpu.HBM), pl.BlockSpec(memory_space=pltpu.VMEM)
    return pl.pallas_call(
        predict_kernel,
        out_shape=[
            jax.ShapeDtypeStruct((parts, members, (oblocks * 128 + rows) // parts + 128), BF16),
            jax.ShapeDtypeStruct((members, 128), F32),
        ],
        in_specs=[pl.BlockSpec(memory_space=pltpu.SMEM)] + [inside] * 5 + [outside],
        out_specs=[outside, inside],
        scratch_shapes=[
            pltpu.VMEM(ops.shape, BF16),
            pltpu.VMEM((2, members, oblocks * 128 // parts), F32),
            pltpu.VMEM((parts, members, oblocks * 128 // parts + 128), BF16),
            pltpu.SemaphoreType.DMA((parts,)),
            pltpu.SemaphoreType.DMA((parts,)),
            pltpu.SemaphoreType.DMA((parts,)),
        ],
        compiler_params=pltpu.CompilerParams(vmem_limit_bytes=50 * 2**20),
        cost_estimate=pl.CostEstimate(flops=2 * ops.size * members, bytes_accessed=2 * ops.size, transcendentals=0),
    )(cols, state, left, right, scaled, inverse, ops)


def gram_kernel(mine_ref, lost_ref, pred_ref, obs_ref, err_ref, out_ref):
    total = pred_ref.shape[0] * pred_ref.shape[1]
    half = total // 2
    width = obs_ref.shape[1]
    given = jnp.concatenate([pred_ref[s : s + 1, :, : width + 128] for s in turned(pred_ref.shape[0])], axis=0).astype(F32)
    parts = given[:, :, width:]
    group = width // 128
    means = parts[:, :group] + parts[:, group : 2 * group] + parts[:, 2 * group : 3 * group]
    means = jnp.concatenate([means[:, o : o + 1] for o in range(group)], axis=2)
    pred = (given[:, :, :width] + means).reshape(total, width)
    mean = jnp.sum(pred, axis=0, keepdims=True) / total
    scale = err_ref[...] * math.sqrt(total - 1)
    white = (pred - mean) / scale
    departure = (obs_ref[...] - mean) / scale
    edge = lax.broadcasted_iota(jnp.int32, (8, width), 0)
    top, low = white[:half], white[half:]
    dot = functools.partial(lax.dot_general, dimension_numbers=NT, precision=HIGHEST, preferred_element_type=F32)
    cross = dot(jnp.where(edge == 0, departure, 0.0), white)[:1]
    members = lost_ref.shape[0]
    member = lax.broadcasted_iota(jnp.int32, (members, total), 0) + mine_ref[0] * members
    own = member == lax.broadcasted_iota(jnp.int32, (members, total), 1)
    lost = jnp.sum(lost_ref[...], axis=1, keepdims=True)
    cross = cross + jnp.sum(jnp.where(own, lost, 0.0), axis=0, keepdims=True)
    first, second = dot(top, top), dot(low, low)
    row = lax.broadcasted_iota(jnp.int32, (half, half), 0)
    col = lax.broadcasted_iota(jnp.int32, (half, half), 1)
    diagonal = jnp.sum(jnp.where(row == col, second, 0.0), axis=0, keepdims=True)
    halves = [dot(low, top), jnp.where(row >= col, first, second)]
    extra = [diagonal, cross[:, :half], cross[:, half:]]
    for i in range(out_ref.shape[0]):
        part = halves[8 * i // half]
        for r in range(8):
            at = (8 * i + r) % half
            out_ref[i, :, 128 * r : 128 * (r + 1)] = part[at : at + 1, :]
        out_ref[i, :, 1024:] = extra[i] if i < len(extra) else jnp.zeros((1, 128), F32)


def gram(mine, lost, shared, obs, err):
    total = shared.shape[0] * shared.shape[1]
    return pl.pallas_call(
        gram_kernel,
        out_shape=jax.ShapeDtypeStruct((total // 8, 1, 1152), F32),
        in_specs=[pl.BlockSpec(memory_space=pltpu.SMEM)] + [pl.BlockSpec(memory_space=pltpu.VMEM)] * 4,
        compiler_params=pltpu.CompilerParams(vmem_limit_bytes=16 * 2**20),
    )(mine, lost, shared, obs, err)


WIDE = 32
STEP = 16


def spread(column):
    return jnp.broadcast_to(column, (8, 128))


def total_of(terms):
    while len(terms) > 1:
        terms = [a + b for a, b in zip(terms[::2], terms[1::2])] + terms[len(terms) & ~1 :]
    return terms[0]


def eliminate(panel, col0):
    groups, span = WIDE // 8, STEP // 8
    sub = lax.broadcasted_iota(jnp.int32, (8, 128), 0)
    tile = col0 // 128
    lanes = lax.broadcasted_iota(jnp.int32, (8, 128), 1) + 128 * tile
    tiles = panel[0].shape[1] // 128
    order = [tile] + [t for t in range(tiles) if t != tile]
    panel = [[p[:, 128 * t : 128 * (t + 1)] for t in range(tiles)] for p in panel]
    out = []
    for q in range(0, groups, span):
        start = col0 + 8 * q
        at = start - 128 * tile
        coef = [[None if g < q else spread(panel[g][tile][:, at + c : at + c + 1]) for g in range(groups)] for c in range(STEP)]
        pivots = [jnp.ones((8, 128), F32) for _ in range(span)]
        for j in range(STEP):
            own, r = q + j // 8, j % 8
            pivot = spread(coef[j][own][r : r + 1, :])
            pivots[j // 8] = jnp.where(sub == r, pivot, pivots[j // 8])
            ratio = 1.0 / pivot
            ahead = [spread(coef[c][own][r : r + 1, :]) for c in range(STEP)]
            for g in range(own, groups):
                times = coef[j][g] * ratio
                if g == own:
                    times = jnp.where(sub > r, times, 0.0)
                for c in [c for c in range(j + 1, STEP)] + [c for c in range(j + 1)]:
                    if c == j:
                        coef[c][g] = jnp.where(sub == r, 1.0, -times) if g == own else -times
                    else:
                        coef[c][g] = coef[c][g] - times * ahead[c]
        inside = (lanes >= start) & (lanes < start + STEP)
        base = []
        for h in range(span):
            unit = jnp.where(lanes - start == sub + 8 * h, 1.0, 0.0)
            base.append([jnp.where(inside, unit, panel[q + h][t]) if t == tile else panel[q + h][t] for t in range(tiles)])
        rows = [[spread(base[c // 8][t][c % 8 : c % 8 + 1, :]) for t in range(tiles)] for c in range(STEP)]
        for g in range(q + span, groups):
            for t in order:
                here = jnp.where(inside, 0.0, panel[g][t]) if t == tile else panel[g][t]
                panel[g][t] = here + total_of([coef[c][g] * rows[c][t] for c in range(STEP)])
        for h in range(span):
            root = lax.rsqrt(pivots[h])
            low = [jnp.where(sub + 8 * h >= c, coef[c][q + h], 0.0) for c in range(min(STEP, 8 * h + 8))]
            out.append([total_of([low[c] * rows[c][t] for c in range(len(low))]) * root for t in range(tiles)])
    return jnp.concatenate([jnp.concatenate(o, axis=1) for o in out], axis=0)


def transform_kernel(gram_ref, ens_ref, out_ref, packed):
    total = 8 * gram_ref.shape[0]
    half = total // 2
    places = turned(out_ref.shape[0])
    first_row = ens_ref.shape[2] - out_ref.shape[2]
    states = jnp.concatenate([ens_ref[s, :, first_row:] for s in places], axis=0).astype(F32)
    mean_state = jnp.sum(states, axis=0, keepdims=True) / total
    anomalies = (states - mean_state).astype(BF16)
    row = lax.broadcasted_iota(jnp.int32, (total, total), 0)
    col = lax.broadcasted_iota(jnp.int32, (total, total), 1)
    for i in range(total // 8):
        for r in range(8):
            packed[8 * i + r : 8 * i + r + 1, :] = gram_ref[i, :, 128 * r : 128 * (r + 1)]
    diagonal, *cross = [gram_ref[i, :, 1024:] for i in range(3)]
    cross = jnp.concatenate(cross, axis=1)
    block, mixed = packed[:half], packed[half:]
    flipped = mixed.T
    above = (row < col)[:half, :half]
    below = (row > col)[:half, :half]
    first = jnp.where(above, flipped, mixed)
    second = jnp.where(above, mixed, jnp.where(below, flipped, diagonal))
    full = jnp.concatenate(
        [jnp.concatenate([first, block.T], axis=1), jnp.concatenate([block, second], axis=1)], axis=0
    )
    full = full + jnp.where(row == col, 1.0, 0.0)
    count = total // WIDE
    blocks = [full[WIDE * t : WIDE * (t + 1), :] for t in range(count)]
    weight = jnp.zeros((1, total), F32)
    for s in range(count):
        r0, r1 = WIDE * s, WIDE * (s + 1)
        done = eliminate([blocks[s][8 * g : 8 * (g + 1), :] for g in range(WIDE // 8)], r0)
        here = col[r0:r1]
        blocks[s] = jnp.where(here <= row[r0:r1], done, 0.0)
        if r1 < total:
            kept = jnp.where((here < r1) & (here > row[r0:r1]), 0.0, done)
            flipped = done.T
            inside = (here >= r0) & (here < r1)
            for t in range(s + 1, count):
                change = jnp.dot(flipped[WIDE * t : WIDE * (t + 1), :], kept, precision=HIGHEST, preferred_element_type=F32)
                blocks[t] = jnp.where(inside, 0.0, blocks[t]) - change
        solved = jnp.sum(blocks[s] * cross, axis=1, keepdims=True)
        weight = weight + jnp.sum(blocks[s] * solved, axis=0, keepdims=True)
    transposed = (jnp.concatenate(blocks, axis=0) + weight).astype(BF16)
    change = jnp.dot(transposed, anomalies, preferred_element_type=F32)
    result = (mean_state + change).astype(BF16)
    members = out_ref.shape[1]
    for i, s in enumerate(places):
        out_ref[s] = result[members * i : members * (i + 1)]


def transform(gram_sum, shared, width):
    sources, members = shared.shape[:2]
    return pl.pallas_call(
        transform_kernel,
        out_shape=jax.ShapeDtypeStruct((sources, members, width), BF16),
        scratch_shapes=[pltpu.VMEM((sources * members, sources * members // 2), F32)],
        compiler_params=pltpu.CompilerParams(vmem_limit_bytes=16 * 2**20),
    )(gram_sum, shared)


def to_all(x, axes, count):
    return lax.all_to_all(jnp.broadcast_to(x[None], (count,) + x.shape), axes, 0, 0, tiled=True)


def local(ensemble, operator_blocks, block_columns, observed, error_scale):
    ens_t = ensemble.T
    members, rows = ens_t.shape
    space_count = lax.axis_size(SPACE)
    member_count = lax.axis_size(MEMBER)
    plane_count = lax.axis_size(PLANE)
    z_count = lax.axis_size("z")
    total = members * member_count
    space_index = lax.axis_index(SPACE)
    member_index = lax.axis_index(MEMBER)
    left = lax.ppermute(ens_t[:, -128:], SPACE, [(i, (i + 1) % space_count) for i in range(space_count)])
    right = lax.ppermute(ens_t[:, :128], SPACE, [((i + 1) % space_count, i) for i in range(space_count)])
    state = jnp.pad(ens_t, ((0, 0), (128, 128)))
    state_local = rows // 128
    cols = jnp.mod(block_columns - space_index * state_local + 1, state_local * space_count)
    inverse = 1.0 / (error_scale * math.sqrt(total - 1))
    scaled = (observed * inverse).reshape(-1, 128)
    shared, lost = predict(cols, state, left, right, scaled, inverse.reshape(-1, 128), operator_blocks, member_count)
    shared = lax.all_to_all(shared, EXCHANGE, 0, 0, tiled=True)
    place = lax.axis_index(EXCHANGE)
    count = observed.shape[0] // member_count
    obs = lax.dynamic_slice_in_dim(observed, place * count, count)[None]
    err = lax.dynamic_slice_in_dim(error_scale, place * count, count)[None]
    part = gram(member_index.astype(jnp.int32).reshape(1), lost, shared, obs, err)
    part = jnp.sum(lax.all_to_all(part, PLANE, 0, 0, tiled=True), axis=0)
    part = jnp.sum(to_all(part, "z", z_count), axis=0)
    gram_sum = to_all(part, PLANE, plane_count).reshape(plane_count, 1, -1)
    analysis = lax.all_to_all(transform(gram_sum, shared, rows // member_count), EXCHANGE, 0, 0, tiled=True)
    return analysis.transpose(1, 0, 2).reshape(members, rows).T


def solution(mesh):
    fine = Mesh(mesh.devices.reshape(16, 2, 4, 4), ("z", "core", "y", "x"))
    in_specs = (P(SPACE, MEMBER), P(SPACE, None, None, None), P(SPACE, None), P(SPACE), P(SPACE))
    return jax.shard_map(local, mesh=fine, in_specs=in_specs, out_specs=P(SPACE, MEMBER), check_vma=False)
```

```python
import functools
import math

import jax
import jax.numpy as jnp
from jax import lax
from jax.experimental import pallas as pl
from jax.experimental.pallas import tpu as pltpu
from jax.sharding import Mesh
from jax.sharding import PartitionSpec as P

F32, BF16 = jnp.float32, jnp.bfloat16
HIGHEST = lax.Precision.HIGHEST
NT = (((1,), (1,)), ((), ()))
TN = (((0,), (0,)), ((), ()))
PLANE = ("core", "y", "x")
MEMBER = ("y", "x")
SPACE = ("z", "core")
EXCHANGE = ("x", "y")


def turned(count):
    side = math.isqrt(count)
    return [i % side * side + i // side for i in range(count)]


def predict_kernel(
    place_ref, cols_ref, state, left_ref, right_ref, scaled_ref, inverse_ref, ops_ref, out_ref, side_ref,
    weights, raw, staged, sems, out_sems, ens_sems,
):
    parts = out_ref.shape[0]
    rows = state.shape[1] - 256
    members = state.shape[0]
    group = ops_ref.shape[0] // parts
    sub = lax.broadcasted_iota(jnp.int32, (members, 128), 0)
    width, share = 128 * group, rows // parts

    def fetch(c):
        return pltpu.make_async_copy(ops_ref.at[pl.ds(c * group, group)], weights.at[pl.ds(c * group, group)], sems.at[c])

    for c in range(4):
        fetch(c).start()
    def deliver(c):
        return pltpu.make_async_copy(staged.at[c], out_ref.at[c, :, pl.ds(0, width + 128)], out_sems.at[c])

    def pass_on(c):
        chunk = state.at[:, pl.ds(pl.multiple_of(128 + c * share, 128), share)]
        return pltpu.make_async_copy(chunk, out_ref.at[c, :, pl.ds(width + 128, share)], ens_sems.at[c])

    def pick(at):
        inner = state[:, pl.ds(pl.multiple_of(at * 128, 128), 128)]
        return jnp.where(at == 0, left_ref[...], jnp.where(at == rows // 128 + 1, right_ref[...], inner))


    def multiply(c):
        values = []
        for o in range(group):
            block = c * group + o
            picked = [pick(cols_ref[block, k]) for k in range(8)]
            rows_of = [weights[block, k] for k in range(8)]
            values.append(
                lax.dot_general(
                    jnp.concatenate(picked, axis=1), jnp.concatenate(rows_of, axis=1), NT, preferred_element_type=F32
                )
            )
        raw[lax.rem(c, 2)] = jnp.concatenate(values, axis=1)

    def split(c, values, lost):
        means = jnp.zeros((members, 128), F32)
        for o in range(group):
            block = c * group + o
            value = values[:, 128 * o : 128 * (o + 1)]
            mean = jnp.sum(value, axis=0, keepdims=True) / members
            rounded = (value - mean).astype(BF16)
            staged[c, :, 128 * o : 128 * (o + 1)] = rounded
            inverse = inverse_ref[pl.ds(block, 1), :]
            departure = scaled_ref[pl.ds(block, 1), :] - mean * inverse
            lost = lost + (value - mean - rounded.astype(F32)) * inverse * departure
            for part in range(3):
                taken = mean.astype(BF16).astype(F32)
                means = jnp.where(sub == group * part + o, taken, means)
                mean = mean - taken
        staged[c, :, width:] = means.astype(BF16)
        deliver(c).start()
        pass_on(c).start()
        return lost

    def body(c, lost):
        fetch(c).wait()

        @pl.when(c + 4 < parts)
        def _():
            fetch(c + 4).start()

        values = raw[lax.rem(c - 1, 2)]
        multiply(c)
        return split(c - 1, values, lost)

    fetch(0).wait()
    fetch(4).start()
    multiply(0)
    lost = lax.fori_loop(1, parts, body, jnp.zeros((members, 128), F32))
    lost = jnp.sum(split(parts - 1, raw[(parts - 1) % 2], lost), axis=1, keepdims=True)
    place, edge = place_ref[0], math.isqrt(parts)
    mine = lax.rem(place, edge) * edge + lax.div(place, edge)
    member = lax.broadcasted_iota(jnp.int32, (members, width), 0) + mine * members
    own = member == lax.broadcasted_iota(jnp.int32, (members, width), 1)
    side_ref[...] = jnp.zeros(side_ref.shape, F32)
    side_ref[2:3, :] = jnp.sum(jnp.where(own, lost, 0.0), axis=0, keepdims=True)
    for o in range(group):
        at = slice(128 * o, 128 * (o + 1))
        side_ref[0:1, at] = scaled_ref[pl.ds(place * group + o, 1), :]
        side_ref[1:2, at] = inverse_ref[pl.ds(place * group + o, 1), :]
    for c in range(parts):
        pass_on(c).wait()
        deliver(c).wait()


def predict(place, cols, state, left, right, scaled, inverse, ops, parts):
    members, rows = state.shape[0], state.shape[1] - 256
    oblocks = ops.shape[0]
    outside, inside = pl.BlockSpec(memory_space=pltpu.HBM), pl.BlockSpec(memory_space=pltpu.VMEM)
    return pl.pallas_call(
        predict_kernel,
        out_shape=[
            jax.ShapeDtypeStruct((parts, members, (oblocks * 128 + rows) // parts + 128), BF16),
            jax.ShapeDtypeStruct((8, oblocks * 128 // parts), F32),
        ],
        in_specs=[pl.BlockSpec(memory_space=pltpu.SMEM)] * 2 + [inside] * 5 + [outside],
        out_specs=[outside, inside],
        scratch_shapes=[
            pltpu.VMEM(ops.shape, BF16),
            pltpu.VMEM((2, members, oblocks * 128 // parts), F32),
            pltpu.VMEM((parts, members, oblocks * 128 // parts + 128), BF16),
            pltpu.SemaphoreType.DMA((parts,)),
            pltpu.SemaphoreType.DMA((parts,)),
            pltpu.SemaphoreType.DMA((parts,)),
        ],
        compiler_params=pltpu.CompilerParams(vmem_limit_bytes=50 * 2**20),
        cost_estimate=pl.CostEstimate(flops=2 * ops.size * members, bytes_accessed=2 * ops.size, transcendentals=0),
    )(place, cols, state, left, right, scaled, inverse, ops)


def gram_kernel(side_ref, pred_ref, out_ref):
    total = pred_ref.shape[0] * pred_ref.shape[1]
    half = total // 2
    width = side_ref.shape[1]
    group = width // 128
    given = jnp.concatenate([pred_ref[s : s + 1, :, : width + 128] for s in turned(pred_ref.shape[0])], axis=0).astype(F32)
    parts = given[:, :, width:]
    means = parts[:, :group] + parts[:, group : 2 * group] + parts[:, 2 * group : 3 * group]
    means = jnp.concatenate([means[:, o : o + 1] for o in range(group)], axis=2)
    pred = (given[:, :, :width] + means).reshape(total, width)
    mean = jnp.sum(pred, axis=0, keepdims=True) / total
    scaled, inverse = side_ref[0:1, :], side_ref[1:2, :]
    white = (pred - mean) * inverse
    departure = scaled - mean * inverse
    edge = lax.broadcasted_iota(jnp.int32, (8, width), 0)
    top, low = white[:half], white[half:]
    dot = functools.partial(lax.dot_general, dimension_numbers=NT, precision=HIGHEST, preferred_element_type=F32)
    cross = dot(jnp.where(edge == 0, departure, 0.0), white)[:1]
    cross = cross + side_ref[2:3, :total]
    first, second = dot(top, top), dot(low, low)
    row = lax.broadcasted_iota(jnp.int32, (half, half), 0)
    col = lax.broadcasted_iota(jnp.int32, (half, half), 1)
    diagonal = jnp.sum(jnp.where(row == col, second, 0.0), axis=0, keepdims=True)
    halves = [dot(low, top), jnp.where(row >= col, first, second)]
    extra = [diagonal, cross[:, :half], cross[:, half:]]
    for i in range(out_ref.shape[0]):
        part = halves[8 * i // half]
        for r in range(8):
            at = (8 * i + r) % half
            out_ref[i, :, 128 * r : 128 * (r + 1)] = part[at : at + 1, :]
        out_ref[i, :, 1024:] = extra[i] if i < len(extra) else jnp.zeros((1, 128), F32)


def gram(side, shared):
    total = shared.shape[0] * shared.shape[1]
    return pl.pallas_call(
        gram_kernel,
        out_shape=jax.ShapeDtypeStruct((total // 8, 1, 1152), F32),
        compiler_params=pltpu.CompilerParams(vmem_limit_bytes=16 * 2**20),
    )(side, shared)


WIDE = 32
STEP = 16


def spread(column):
    return jnp.broadcast_to(column, (8, 128))


def total_of(terms):
    while len(terms) > 1:
        terms = [a + b for a, b in zip(terms[::2], terms[1::2])] + terms[len(terms) & ~1 :]
    return terms[0]


def eliminate(panel, col0):
    groups, span = WIDE // 8, STEP // 8
    sub = lax.broadcasted_iota(jnp.int32, (8, 128), 0)
    tile = col0 // 128
    lanes = lax.broadcasted_iota(jnp.int32, (8, 128), 1) + 128 * tile
    tiles = panel[0].shape[1] // 128
    order = [tile] + [t for t in range(tiles) if t != tile]
    panel = [[p[:, 128 * t : 128 * (t + 1)] for t in range(tiles)] for p in panel]
    out = []
    for q in range(0, groups, span):
        start = col0 + 8 * q
        at = start - 128 * tile
        coef = [[None if g < q else spread(panel[g][tile][:, at + c : at + c + 1]) for g in range(groups)] for c in range(STEP)]
        pivots = [jnp.ones((8, 128), F32) for _ in range(span)]
        for j in range(STEP):
            own, r = q + j // 8, j % 8
            pivot = spread(coef[j][own][r : r + 1, :])
            pivots[j // 8] = jnp.where(sub == r, pivot, pivots[j // 8])
            ratio = 1.0 / pivot
            ahead = [spread(coef[c][own][r : r + 1, :]) for c in range(STEP)]
            for g in range(own, groups):
                times = coef[j][g] * ratio
                if g == own:
                    times = jnp.where(sub > r, times, 0.0)
                for c in [c for c in range(j + 1, STEP)] + [c for c in range(j + 1)]:
                    if c == j:
                        coef[c][g] = jnp.where(sub == r, 1.0, -times) if g == own else -times
                    else:
                        coef[c][g] = coef[c][g] - times * ahead[c]
        inside = (lanes >= start) & (lanes < start + STEP)
        base = []
        for h in range(span):
            unit = jnp.where(lanes - start == sub + 8 * h, 1.0, 0.0)
            base.append([jnp.where(inside, unit, panel[q + h][t]) if t == tile else panel[q + h][t] for t in range(tiles)])
        rows = [[spread(base[c // 8][t][c % 8 : c % 8 + 1, :]) for t in range(tiles)] for c in range(STEP)]
        for g in range(q + span, groups):
            for t in order:
                here = jnp.where(inside, 0.0, panel[g][t]) if t == tile else panel[g][t]
                panel[g][t] = here + total_of([coef[c][g] * rows[c][t] for c in range(STEP)])
        for h in range(span):
            root = lax.rsqrt(pivots[h])
            low = [jnp.where(sub + 8 * h >= c, coef[c][q + h], 0.0) for c in range(min(STEP, 8 * h + 8))]
            out.append([total_of([low[c] * rows[c][t] for c in range(len(low))]) * root for t in range(tiles)])
    return jnp.concatenate([jnp.concatenate(o, axis=1) for o in out], axis=0)


def transform_kernel(gram_ref, ens_ref, out_ref, packed):
    total = 8 * gram_ref.shape[0]
    half = total // 2
    places = turned(out_ref.shape[0])
    first_row = ens_ref.shape[2] - out_ref.shape[2]
    states = jnp.concatenate([ens_ref[s, :, first_row:] for s in places], axis=0).astype(F32)
    mean_state = jnp.sum(states, axis=0, keepdims=True) / total
    anomalies = (states - mean_state).astype(BF16)
    row = lax.broadcasted_iota(jnp.int32, (total, total), 0)
    col = lax.broadcasted_iota(jnp.int32, (total, total), 1)
    for i in range(total // 8):
        for r in range(8):
            packed[8 * i + r : 8 * i + r + 1, :] = gram_ref[i, :, 128 * r : 128 * (r + 1)]
    diagonal, *cross = [gram_ref[i, :, 1024:] for i in range(3)]
    cross = jnp.concatenate(cross, axis=1)
    block, mixed = packed[:half], packed[half:]
    flipped = mixed.T
    above = (row < col)[:half, :half]
    below = (row > col)[:half, :half]
    first = jnp.where(above, flipped, mixed)
    second = jnp.where(above, mixed, jnp.where(below, flipped, diagonal))
    full = jnp.concatenate(
        [jnp.concatenate([first, block.T], axis=1), jnp.concatenate([block, second], axis=1)], axis=0
    )
    full = full + jnp.where(row == col, 1.0, 0.0)
    count = total // WIDE
    blocks = [full[WIDE * t : WIDE * (t + 1), :] for t in range(count)]
    weight = jnp.zeros((1, total), F32)
    for s in range(count):
        r0, r1 = WIDE * s, WIDE * (s + 1)
        done = eliminate([blocks[s][8 * g : 8 * (g + 1), :] for g in range(WIDE // 8)], r0)
        here = col[r0:r1]
        blocks[s] = jnp.where(here <= row[r0:r1], done, 0.0)
        if r1 < total:
            kept = jnp.where((here < r1) & (here > row[r0:r1]), 0.0, done)
            flipped = done.T
            inside = (here >= r0) & (here < r1)
            for t in range(s + 1, count):
                change = jnp.dot(flipped[WIDE * t : WIDE * (t + 1), :], kept, precision=HIGHEST, preferred_element_type=F32)
                blocks[t] = jnp.where(inside, 0.0, blocks[t]) - change
        solved = jnp.sum(blocks[s] * cross, axis=1, keepdims=True)
        weight = weight + jnp.sum(blocks[s] * solved, axis=0, keepdims=True)
    transposed = (jnp.concatenate(blocks, axis=0) + weight).astype(BF16)
    change = jnp.dot(transposed, anomalies, preferred_element_type=F32)
    result = (mean_state + change).astype(BF16)
    members = out_ref.shape[1]
    for i, s in enumerate(places):
        out_ref[s] = result[members * i : members * (i + 1)]


def transform(gram_sum, shared, width):
    sources, members = shared.shape[:2]
    return pl.pallas_call(
        transform_kernel,
        out_shape=jax.ShapeDtypeStruct((sources, members, width), BF16),
        scratch_shapes=[pltpu.VMEM((sources * members, sources * members // 2), F32)],
        compiler_params=pltpu.CompilerParams(vmem_limit_bytes=16 * 2**20),
    )(gram_sum, shared)


def to_all(x, axes, count):
    return lax.all_to_all(jnp.broadcast_to(x[None], (count,) + x.shape), axes, 0, 0, tiled=True)


def local(ensemble, operator_blocks, block_columns, observed, error_scale):
    ens_t = ensemble.T
    members, rows = ens_t.shape
    space_count = lax.axis_size(SPACE)
    member_count = lax.axis_size(MEMBER)
    plane_count = lax.axis_size(PLANE)
    z_count = lax.axis_size("z")
    total = members * member_count
    space_index = lax.axis_index(SPACE)
    left = lax.ppermute(ens_t[:, -128:], SPACE, [(i, (i + 1) % space_count) for i in range(space_count)])
    right = lax.ppermute(ens_t[:, :128], SPACE, [((i + 1) % space_count, i) for i in range(space_count)])
    state = jnp.pad(ens_t, ((0, 0), (128, 128)))
    state_local = rows // 128
    cols = jnp.mod(block_columns - space_index * state_local + 1, state_local * space_count)
    inverse = 1.0 / (error_scale * math.sqrt(total - 1))
    scaled, inverse = (observed * inverse).reshape(-1, 128), inverse.reshape(-1, 128)
    place = lax.axis_index(EXCHANGE).astype(jnp.int32).reshape(1)
    shared, side = predict(place, cols, state, left, right, scaled, inverse, operator_blocks, member_count)
    shared = lax.all_to_all(shared, EXCHANGE, 0, 0, tiled=True)
    part = gram(side, shared)
    part = jnp.sum(lax.all_to_all(part, PLANE, 0, 0, tiled=True), axis=0)
    part = jnp.sum(to_all(part, "z", z_count), axis=0)
    gram_sum = to_all(part, PLANE, plane_count).reshape(plane_count, 1, -1)
    analysis = lax.all_to_all(transform(gram_sum, shared, rows // member_count), EXCHANGE, 0, 0, tiled=True)
    return analysis.transpose(1, 0, 2).reshape(members, rows).T


def solution(mesh):
    fine = Mesh(mesh.devices.reshape(16, 2, 4, 4), ("z", "core", "y", "x"))
    in_specs = (P(SPACE, MEMBER), P(SPACE, None, None, None), P(SPACE, None), P(SPACE), P(SPACE))
    return jax.shard_map(local, mesh=fine, in_specs=in_specs, out_specs=P(SPACE, MEMBER), check_vma=False)
```

```python
import functools
import math

import jax
import jax.numpy as jnp
from jax import lax
from jax.experimental import pallas as pl
from jax.experimental.pallas import tpu as pltpu
from jax.sharding import Mesh
from jax.sharding import PartitionSpec as P

F32, BF16 = jnp.float32, jnp.bfloat16
HIGHEST = lax.Precision.HIGHEST
NT = (((1,), (1,)), ((), ()))
TN = (((0,), (0,)), ((), ()))
PLANE = ("core", "y", "x")
MEMBER = ("y", "x")
SPACE = ("z", "core")


def predict_kernel(
    place_ref, cols_ref, state, left_ref, right_ref, scaled_ref, inverse_ref, ops_ref, out_ref, side_ref,
    weights, raw, staged, sems, out_sems, ens_sems,
):
    parts = out_ref.shape[0]
    rows = state.shape[1] - 256
    members = state.shape[0]
    group = ops_ref.shape[0] // parts
    sub = lax.broadcasted_iota(jnp.int32, (members, 128), 0)
    width, share = 128 * group, rows // parts

    def fetch(c):
        return pltpu.make_async_copy(ops_ref.at[pl.ds(c * group, group)], weights.at[pl.ds(c * group, group)], sems.at[c])

    for c in range(4):
        fetch(c).start()
    def deliver(c):
        return pltpu.make_async_copy(staged.at[c], out_ref.at[c, :, pl.ds(0, width + 128)], out_sems.at[c])

    def pass_on(c):
        chunk = state.at[:, pl.ds(pl.multiple_of(128 + c * share, 128), share)]
        return pltpu.make_async_copy(chunk, out_ref.at[c, :, pl.ds(width + 128, share)], ens_sems.at[c])

    def pick(at):
        inner = state[:, pl.ds(pl.multiple_of(at * 128, 128), 128)]
        return jnp.where(at == 0, left_ref[...], jnp.where(at == rows // 128 + 1, right_ref[...], inner))


    def multiply(c):
        values = []
        for o in range(group):
            block = c * group + o
            picked = [pick(cols_ref[block, k]) for k in range(8)]
            rows_of = [weights[block, k] for k in range(8)]
            values.append(
                lax.dot_general(
                    jnp.concatenate(picked, axis=1), jnp.concatenate(rows_of, axis=1), NT, preferred_element_type=F32
                )
            )
        raw[lax.rem(c, 2)] = jnp.concatenate(values, axis=1)

    def split(c, values, lost):
        means = jnp.zeros((members, 128), F32)
        for o in range(group):
            block = c * group + o
            value = values[:, 128 * o : 128 * (o + 1)]
            mean = jnp.sum(value, axis=0, keepdims=True) / members
            rounded = (value - mean).astype(BF16)
            staged[c, :, 128 * o : 128 * (o + 1)] = rounded
            inverse = inverse_ref[pl.ds(block, 1), :]
            departure = scaled_ref[pl.ds(block, 1), :] - mean * inverse
            lost = lost + (value - mean - rounded.astype(F32)) * inverse * departure
            for part in range(3):
                taken = mean.astype(BF16).astype(F32)
                means = jnp.where(sub == group * part + o, taken, means)
                mean = mean - taken
        staged[c, :, width:] = means.astype(BF16)
        deliver(c).start()
        pass_on(c).start()
        return lost

    def body(c, lost):
        fetch(c).wait()

        @pl.when(c + 4 < parts)
        def _():
            fetch(c + 4).start()

        values = raw[lax.rem(c - 1, 2)]
        multiply(c)
        return split(c - 1, values, lost)

    fetch(0).wait()
    fetch(4).start()
    multiply(0)
    lost = lax.fori_loop(1, parts, body, jnp.zeros((members, 128), F32))
    lost = jnp.sum(split(parts - 1, raw[(parts - 1) % 2], lost), axis=1, keepdims=True)
    place = place_ref[0]
    member = lax.broadcasted_iota(jnp.int32, (members, width), 0) + place * members
    own = member == lax.broadcasted_iota(jnp.int32, (members, width), 1)
    side_ref[...] = jnp.zeros(side_ref.shape, F32)
    side_ref[2:3, :] = jnp.sum(jnp.where(own, lost, 0.0), axis=0, keepdims=True)
    for o in range(group):
        at = slice(128 * o, 128 * (o + 1))
        side_ref[0:1, at] = scaled_ref[pl.ds(place * group + o, 1), :]
        side_ref[1:2, at] = inverse_ref[pl.ds(place * group + o, 1), :]
    for c in range(parts):
        pass_on(c).wait()
        deliver(c).wait()


def predict(place, cols, state, left, right, scaled, inverse, ops, parts):
    members, rows = state.shape[0], state.shape[1] - 256
    oblocks = ops.shape[0]
    outside, inside = pl.BlockSpec(memory_space=pltpu.HBM), pl.BlockSpec(memory_space=pltpu.VMEM)
    return pl.pallas_call(
        predict_kernel,
        out_shape=[
            jax.ShapeDtypeStruct((parts, members, (oblocks * 128 + rows) // parts + 128), BF16),
            jax.ShapeDtypeStruct((8, oblocks * 128 // parts), F32),
        ],
        in_specs=[pl.BlockSpec(memory_space=pltpu.SMEM)] * 2 + [inside] * 5 + [outside],
        out_specs=[outside, inside],
        scratch_shapes=[
            pltpu.VMEM(ops.shape, BF16),
            pltpu.VMEM((2, members, oblocks * 128 // parts), F32),
            pltpu.VMEM((parts, members, oblocks * 128 // parts + 128), BF16),
            pltpu.SemaphoreType.DMA((parts,)),
            pltpu.SemaphoreType.DMA((parts,)),
            pltpu.SemaphoreType.DMA((parts,)),
        ],
        compiler_params=pltpu.CompilerParams(vmem_limit_bytes=50 * 2**20),
        cost_estimate=pl.CostEstimate(flops=2 * ops.size * members, bytes_accessed=2 * ops.size, transcendentals=0),
    )(place, cols, state, left, right, scaled, inverse, ops)


def gram_kernel(side_ref, pred_ref, out_ref):
    total = pred_ref.shape[0] * pred_ref.shape[1]
    half = total // 2
    width = side_ref.shape[1]
    group = width // 128
    given = pred_ref[:, :, : width + 128].astype(F32)
    parts = given[:, :, width:]
    means = parts[:, :group] + parts[:, group : 2 * group] + parts[:, 2 * group : 3 * group]
    means = jnp.concatenate([means[:, o : o + 1] for o in range(group)], axis=2)
    pred = (given[:, :, :width] + means).reshape(total, width)
    mean = jnp.sum(pred, axis=0, keepdims=True) / total
    scaled, inverse = side_ref[0:1, :], side_ref[1:2, :]
    white = (pred - mean) * inverse
    departure = scaled - mean * inverse
    edge = lax.broadcasted_iota(jnp.int32, (8, width), 0)
    top, low = white[:half], white[half:]
    dot = functools.partial(lax.dot_general, dimension_numbers=NT, precision=HIGHEST, preferred_element_type=F32)
    cross = dot(jnp.where(edge == 0, departure, 0.0), white)[:1]
    cross = cross + side_ref[2:3, :total]
    first, second = dot(top, top), dot(low, low)
    row = lax.broadcasted_iota(jnp.int32, (half, half), 0)
    col = lax.broadcasted_iota(jnp.int32, (half, half), 1)
    diagonal = jnp.sum(jnp.where(row == col, second, 0.0), axis=0, keepdims=True)
    halves = [dot(low, top), jnp.where(row >= col, first, second)]
    extra = [diagonal, cross[:, :half], cross[:, half:]]
    for i in range(out_ref.shape[0]):
        part = halves[8 * i // half]
        for r in range(8):
            at = (8 * i + r) % half
            out_ref[i, :, 128 * r : 128 * (r + 1)] = part[at : at + 1, :]
        out_ref[i, :, 1024:] = extra[i] if i < len(extra) else jnp.zeros((1, 128), F32)


def gram(side, shared):
    total = shared.shape[0] * shared.shape[1]
    return pl.pallas_call(
        gram_kernel,
        out_shape=jax.ShapeDtypeStruct((total // 8, 1, 1152), F32),
        compiler_params=pltpu.CompilerParams(vmem_limit_bytes=16 * 2**20),
    )(side, shared)


WIDE = 32
STEP = 16


def spread(column):
    return jnp.broadcast_to(column, (8, 128))


def total_of(terms):
    while len(terms) > 1:
        terms = [a + b for a, b in zip(terms[::2], terms[1::2])] + terms[len(terms) & ~1 :]
    return terms[0]


def eliminate(panel, col0):
    groups, span = WIDE // 8, STEP // 8
    sub = lax.broadcasted_iota(jnp.int32, (8, 128), 0)
    tile = col0 // 128
    lanes = lax.broadcasted_iota(jnp.int32, (8, 128), 1) + 128 * tile
    tiles = panel[0].shape[1] // 128
    order = [tile] + [t for t in range(tiles) if t != tile]
    panel = [[p[:, 128 * t : 128 * (t + 1)] for t in range(tiles)] for p in panel]
    out = []
    for q in range(0, groups, span):
        start = col0 + 8 * q
        at = start - 128 * tile
        coef = [[None if g < q else spread(panel[g][tile][:, at + c : at + c + 1]) for g in range(groups)] for c in range(STEP)]
        pivots = [jnp.ones((8, 128), F32) for _ in range(span)]
        for j in range(STEP):
            own, r = q + j // 8, j % 8
            pivot = spread(coef[j][own][r : r + 1, :])
            pivots[j // 8] = jnp.where(sub == r, pivot, pivots[j // 8])
            ratio = 1.0 / pivot
            ahead = [spread(coef[c][own][r : r + 1, :]) for c in range(STEP)]
            for g in range(own, groups):
                times = coef[j][g] * ratio
                if g == own:
                    times = jnp.where(sub > r, times, 0.0)
                for c in [c for c in range(j + 1, STEP)] + [c for c in range(j + 1)]:
                    if c == j:
                        coef[c][g] = jnp.where(sub == r, 1.0, -times) if g == own else -times
                    else:
                        coef[c][g] = coef[c][g] - times * ahead[c]
        inside = (lanes >= start) & (lanes < start + STEP)
        base = []
        for h in range(span):
            unit = jnp.where(lanes - start == sub + 8 * h, 1.0, 0.0)
            base.append([jnp.where(inside, unit, panel[q + h][t]) if t == tile else panel[q + h][t] for t in range(tiles)])
        rows = [[spread(base[c // 8][t][c % 8 : c % 8 + 1, :]) for t in range(tiles)] for c in range(STEP)]
        for g in range(q + span, groups):
            for t in order:
                here = jnp.where(inside, 0.0, panel[g][t]) if t == tile else panel[g][t]
                panel[g][t] = here + total_of([coef[c][g] * rows[c][t] for c in range(STEP)])
        for h in range(span):
            root = lax.rsqrt(pivots[h])
            low = [jnp.where(sub + 8 * h >= c, coef[c][q + h], 0.0) for c in range(min(STEP, 8 * h + 8))]
            out.append([total_of([low[c] * rows[c][t] for c in range(len(low))]) * root for t in range(tiles)])
    return jnp.concatenate([jnp.concatenate(o, axis=1) for o in out], axis=0)


def transform_kernel(gram_ref, ens_ref, out_ref, packed):
    total = 8 * gram_ref.shape[0]
    half = total // 2
    first_row = ens_ref.shape[2] - out_ref.shape[2]
    states = ens_ref[:, :, first_row:].astype(F32).reshape(total, -1)
    mean_state = jnp.sum(states, axis=0, keepdims=True) / total
    anomalies = (states - mean_state).astype(BF16)
    row = lax.broadcasted_iota(jnp.int32, (total, total), 0)
    col = lax.broadcasted_iota(jnp.int32, (total, total), 1)
    for i in range(total // 8):
        for r in range(8):
            packed[8 * i + r : 8 * i + r + 1, :] = gram_ref[i, :, 128 * r : 128 * (r + 1)]
    diagonal, *cross = [gram_ref[i, :, 1024:] for i in range(3)]
    cross = jnp.concatenate(cross, axis=1)
    block, mixed = packed[:half], packed[half:]
    flipped = mixed.T
    above = (row < col)[:half, :half]
    below = (row > col)[:half, :half]
    first = jnp.where(above, flipped, mixed)
    second = jnp.where(above, mixed, jnp.where(below, flipped, diagonal))
    full = jnp.concatenate(
        [jnp.concatenate([first, block.T], axis=1), jnp.concatenate([block, second], axis=1)], axis=0
    )
    full = full + jnp.where(row == col, 1.0, 0.0)
    count = total // WIDE
    blocks = [full[WIDE * t : WIDE * (t + 1), :] for t in range(count)]
    weight = jnp.zeros((1, total), F32)
    for s in range(count):
        r0, r1 = WIDE * s, WIDE * (s + 1)
        done = eliminate([blocks[s][8 * g : 8 * (g + 1), :] for g in range(WIDE // 8)], r0)
        here = col[r0:r1]
        blocks[s] = jnp.where(here <= row[r0:r1], done, 0.0)
        if r1 < total:
            kept = jnp.where((here < r1) & (here > row[r0:r1]), 0.0, done)
            flipped = done.T
            inside = (here >= r0) & (here < r1)
            for t in range(s + 1, count):
                change = jnp.dot(flipped[WIDE * t : WIDE * (t + 1), :], kept, precision=HIGHEST, preferred_element_type=F32)
                blocks[t] = jnp.where(inside, 0.0, blocks[t]) - change
        solved = jnp.sum(blocks[s] * cross, axis=1, keepdims=True)
        weight = weight + jnp.sum(blocks[s] * solved, axis=0, keepdims=True)
    transposed = (jnp.concatenate(blocks, axis=0) + weight).astype(BF16)
    change = jnp.dot(transposed, anomalies, preferred_element_type=F32)
    out_ref[...] = (mean_state + change).astype(BF16).reshape(out_ref.shape)


def transform(gram_sum, shared, width):
    sources, members = shared.shape[:2]
    return pl.pallas_call(
        transform_kernel,
        out_shape=jax.ShapeDtypeStruct((sources, members, width), BF16),
        scratch_shapes=[pltpu.VMEM((sources * members, sources * members // 2), F32)],
        compiler_params=pltpu.CompilerParams(vmem_limit_bytes=16 * 2**20),
    )(gram_sum, shared)


def to_all(x, axes, count):
    return lax.all_to_all(jnp.broadcast_to(x[None], (count,) + x.shape), axes, 0, 0, tiled=True)


def local(ensemble, operator_blocks, block_columns, observed, error_scale):
    ens_t = ensemble.T
    members, rows = ens_t.shape
    space_count = lax.axis_size(SPACE)
    member_count = lax.axis_size(MEMBER)
    plane_count = lax.axis_size(PLANE)
    z_count = lax.axis_size("z")
    total = members * member_count
    space_index = lax.axis_index(SPACE)
    left = lax.ppermute(ens_t[:, -128:], SPACE, [(i, (i + 1) % space_count) for i in range(space_count)])
    right = lax.ppermute(ens_t[:, :128], SPACE, [((i + 1) % space_count, i) for i in range(space_count)])
    state = jnp.pad(ens_t, ((0, 0), (128, 128)))
    state_local = rows // 128
    cols = jnp.mod(block_columns - space_index * state_local + 1, state_local * space_count)
    inverse = 1.0 / (error_scale * math.sqrt(total - 1))
    scaled, inverse = (observed * inverse).reshape(-1, 128), inverse.reshape(-1, 128)
    place = lax.axis_index(MEMBER).astype(jnp.int32).reshape(1)
    shared, side = predict(place, cols, state, left, right, scaled, inverse, operator_blocks, member_count)
    shared = lax.all_to_all(shared, MEMBER, 0, 0, tiled=True)
    part = gram(side, shared)
    part = jnp.sum(lax.all_to_all(part, PLANE, 0, 0, tiled=True), axis=0)
    part = jnp.sum(to_all(part, "z", z_count), axis=0)
    gram_sum = to_all(part, PLANE, plane_count).reshape(plane_count, 1, -1)
    analysis = lax.all_to_all(transform(gram_sum, shared, rows // member_count), MEMBER, 0, 0, tiled=True)
    return analysis.transpose(1, 0, 2).reshape(members, rows).T


def solution(mesh):
    fine = Mesh(mesh.devices.reshape(16, 2, 4, 4), ("z", "core", "y", "x"))
    in_specs = (P(SPACE, MEMBER), P(SPACE, None, None, None), P(SPACE, None), P(SPACE), P(SPACE))
    return jax.shard_map(local, mesh=fine, in_specs=in_specs, out_specs=P(SPACE, MEMBER), check_vma=False)
```

```python
import functools
import math

import jax
import jax.numpy as jnp
from jax import lax
from jax.experimental import pallas as pl
from jax.experimental.pallas import tpu as pltpu
from jax.sharding import Mesh
from jax.sharding import PartitionSpec as P

F32, BF16 = jnp.float32, jnp.bfloat16
HIGHEST = lax.Precision.HIGHEST
NT = (((1,), (1,)), ((), ()))
TN = (((0,), (0,)), ((), ()))
PLANE = ("core", "y", "x")
MEMBER = ("y", "x")
SPACE = ("z", "core")
EXCHANGE = ("x", "y")


def turned(count):
    side = math.isqrt(count)
    return [i % side * side + i // side for i in range(count)]


def predict_kernel(
    place_ref, cols_ref, state, right_ref, left_ref, scaled_ref, inverse_ref, ops_ref, out_ref, side_ref,
    weights, raw, staged, sems, out_sems, ens_sems,
):
    parts = out_ref.shape[0]
    rows = state.shape[1] - 256
    members = state.shape[0]
    group = ops_ref.shape[0] // parts
    sub = lax.broadcasted_iota(jnp.int32, (members, 128), 0)
    width, share = 128 * group, rows // parts

    def fetch(c):
        return pltpu.make_async_copy(ops_ref.at[pl.ds(c * group, group)], weights.at[pl.ds(c * group, group)], sems.at[c])

    for c in range(4):
        fetch(c).start()
    def deliver(c):
        return pltpu.make_async_copy(staged.at[c], out_ref.at[c, :, pl.ds(0, width + 128)], out_sems.at[c])

    def pass_on(c):
        chunk = state.at[:, pl.ds(pl.multiple_of(128 + c * share, 128), share)]
        return pltpu.make_async_copy(chunk, out_ref.at[c, :, pl.ds(width + 128, share)], ens_sems.at[c])

    def pick(at):
        inner = state[:, pl.ds(pl.multiple_of(at * 128, 128), 128)]
        return jnp.where(at == 0, left_ref[...], jnp.where(at == rows // 128 + 1, right_ref[...], inner))


    def multiply(c):
        values = []
        for o in range(group):
            block = c * group + o
            picked = [pick(cols_ref[block, k]) for k in range(8)]
            rows_of = [weights[block, k] for k in range(8)]
            values.append(
                lax.dot_general(
                    jnp.concatenate(picked, axis=1), jnp.concatenate(rows_of, axis=1), NT, preferred_element_type=F32
                )
            )
        raw[lax.rem(c, 2)] = jnp.concatenate(values, axis=1)

    def split(c, values, lost):
        means = jnp.zeros((members, 128), F32)
        for o in range(group):
            block = c * group + o
            value = values[:, 128 * o : 128 * (o + 1)]
            mean = jnp.sum(value, axis=0, keepdims=True) / members
            rounded = (value - mean).astype(BF16)
            staged[c, :, 128 * o : 128 * (o + 1)] = rounded
            inverse = inverse_ref[pl.ds(block, 1), :]
            departure = scaled_ref[pl.ds(block, 1), :] - mean * inverse
            lost = lost + (value - mean - rounded.astype(F32)) * inverse * departure
            for part in range(3):
                taken = mean.astype(BF16).astype(F32)
                means = jnp.where(sub == group * part + o, taken, means)
                mean = mean - taken
        staged[c, :, width:] = means.astype(BF16)
        deliver(c).start()
        pass_on(c).start()
        return lost

    def body(c, lost):
        fetch(c).wait()

        @pl.when(c + 4 < parts)
        def _():
            fetch(c + 4).start()

        values = raw[lax.rem(c - 1, 2)]
        multiply(c)
        return split(c - 1, values, lost)

    fetch(0).wait()
    fetch(4).start()
    multiply(0)
    lost = lax.fori_loop(1, parts, body, jnp.zeros((members, 128), F32))
    lost = jnp.sum(split(parts - 1, raw[(parts - 1) % 2], lost), axis=1, keepdims=True)
    place, edge = place_ref[0], math.isqrt(parts)
    mine = lax.rem(place, edge) * edge + lax.div(place, edge)
    member = lax.broadcasted_iota(jnp.int32, (members, width), 0) + mine * members
    own = member == lax.broadcasted_iota(jnp.int32, (members, width), 1)
    side_ref[...] = jnp.zeros(side_ref.shape, F32)
    side_ref[2:3, :] = jnp.sum(jnp.where(own, lost, 0.0), axis=0, keepdims=True)
    for o in range(group):
        at = slice(128 * o, 128 * (o + 1))
        side_ref[0:1, at] = scaled_ref[pl.ds(place * group + o, 1), :]
        side_ref[1:2, at] = inverse_ref[pl.ds(place * group + o, 1), :]
    for c in range(parts):
        pass_on(c).wait()
        deliver(c).wait()


def predict(place, cols, state, left, right, scaled, inverse, ops, parts):
    members, rows = state.shape[0], state.shape[1] - 256
    oblocks = ops.shape[0]
    outside, inside = pl.BlockSpec(memory_space=pltpu.HBM), pl.BlockSpec(memory_space=pltpu.VMEM)
    return pl.pallas_call(
        predict_kernel,
        out_shape=[
            jax.ShapeDtypeStruct((parts, members, (oblocks * 128 + rows) // parts + 128), BF16),
            jax.ShapeDtypeStruct((8, oblocks * 128 // parts), F32),
        ],
        in_specs=[pl.BlockSpec(memory_space=pltpu.SMEM)] * 2 + [inside] * 5 + [outside],
        out_specs=[outside, inside],
        scratch_shapes=[
            pltpu.VMEM(ops.shape, BF16),
            pltpu.VMEM((2, members, oblocks * 128 // parts), F32),
            pltpu.VMEM((parts, members, oblocks * 128 // parts + 128), BF16),
            pltpu.SemaphoreType.DMA((parts,)),
            pltpu.SemaphoreType.DMA((parts,)),
            pltpu.SemaphoreType.DMA((parts,)),
        ],
        compiler_params=pltpu.CompilerParams(vmem_limit_bytes=50 * 2**20),
        cost_estimate=pl.CostEstimate(flops=2 * ops.size * members, bytes_accessed=2 * ops.size, transcendentals=0),
    )(place, cols, state, right, left, scaled, inverse, ops)


def gram_kernel(side_ref, pred_ref, out_ref):
    total = pred_ref.shape[0] * pred_ref.shape[1]
    half = total // 2
    width = side_ref.shape[1]
    group = width // 128
    given = jnp.concatenate([pred_ref[s : s + 1, :, : width + 128] for s in turned(pred_ref.shape[0])], axis=0).astype(F32)
    parts = given[:, :, width:]
    means = parts[:, :group] + parts[:, group : 2 * group] + parts[:, 2 * group : 3 * group]
    means = jnp.concatenate([means[:, o : o + 1] for o in range(group)], axis=2)
    pred = (given[:, :, :width] + means).reshape(total, width)
    mean = jnp.sum(pred, axis=0, keepdims=True) / total
    scaled, inverse = side_ref[0:1, :], side_ref[1:2, :]
    white = (pred - mean) * inverse
    departure = scaled - mean * inverse
    edge = lax.broadcasted_iota(jnp.int32, (8, width), 0)
    top, low = white[:half], white[half:]
    dot = functools.partial(lax.dot_general, dimension_numbers=NT, precision=HIGHEST, preferred_element_type=F32)
    cross = dot(jnp.where(edge == 0, departure, 0.0), white)[:1]
    cross = cross + side_ref[2:3, :total]
    first, second = dot(top, top), dot(low, low)
    row = lax.broadcasted_iota(jnp.int32, (half, half), 0)
    col = lax.broadcasted_iota(jnp.int32, (half, half), 1)
    diagonal = jnp.sum(jnp.where(row == col, second, 0.0), axis=0, keepdims=True)
    halves = [dot(low, top), jnp.where(row >= col, first, second)]
    extra = [diagonal, cross[:, :half], cross[:, half:]]
    for i in range(out_ref.shape[0]):
        part = halves[8 * i // half]
        for r in range(8):
            at = (8 * i + r) % half
            out_ref[i, :, 128 * r : 128 * (r + 1)] = part[at : at + 1, :]
        out_ref[i, :, 1024:] = extra[i] if i < len(extra) else jnp.zeros((1, 128), F32)


def gram(side, shared):
    total = shared.shape[0] * shared.shape[1]
    return pl.pallas_call(
        gram_kernel,
        out_shape=jax.ShapeDtypeStruct((total // 8, 1, 1152), F32),
        compiler_params=pltpu.CompilerParams(vmem_limit_bytes=16 * 2**20),
    )(side, shared)


WIDE = 32
STEP = 16


def spread(column):
    return jnp.broadcast_to(column, (8, 128))


def total_of(terms):
    while len(terms) > 1:
        terms = [a + b for a, b in zip(terms[::2], terms[1::2])] + terms[len(terms) & ~1 :]
    return terms[0]


def eliminate(panel, col0):
    groups, span = WIDE // 8, STEP // 8
    sub = lax.broadcasted_iota(jnp.int32, (8, 128), 0)
    tile = col0 // 128
    lanes = lax.broadcasted_iota(jnp.int32, (8, 128), 1) + 128 * tile
    tiles = panel[0].shape[1] // 128
    order = [tile] + [t for t in range(tiles) if t != tile]
    panel = [[p[:, 128 * t : 128 * (t + 1)] for t in range(tiles)] for p in panel]
    out = []
    for q in range(0, groups, span):
        start = col0 + 8 * q
        at = start - 128 * tile
        coef = [[None if g < q else spread(panel[g][tile][:, at + c : at + c + 1]) for g in range(groups)] for c in range(STEP)]
        pivots = [jnp.ones((8, 128), F32) for _ in range(span)]
        for j in range(STEP):
            own, r = q + j // 8, j % 8
            pivot = spread(coef[j][own][r : r + 1, :])
            pivots[j // 8] = jnp.where(sub == r, pivot, pivots[j // 8])
            ratio = 1.0 / pivot
            ahead = [spread(coef[c][own][r : r + 1, :]) for c in range(STEP)]
            for g in range(own, groups):
                times = coef[j][g] * ratio
                if g == own:
                    times = jnp.where(sub > r, times, 0.0)
                for c in [c for c in range(j + 1, STEP)] + [c for c in range(j + 1)]:
                    if c == j:
                        coef[c][g] = jnp.where(sub == r, 1.0, -times) if g == own else -times
                    else:
                        coef[c][g] = coef[c][g] - times * ahead[c]
        inside = (lanes >= start) & (lanes < start + STEP)
        base = []
        for h in range(span):
            unit = jnp.where(lanes - start == sub + 8 * h, 1.0, 0.0)
            base.append([jnp.where(inside, unit, panel[q + h][t]) if t == tile else panel[q + h][t] for t in range(tiles)])
        rows = [[spread(base[c // 8][t][c % 8 : c % 8 + 1, :]) for t in range(tiles)] for c in range(STEP)]
        for g in range(q + span, groups):
            for t in order:
                here = jnp.where(inside, 0.0, panel[g][t]) if t == tile else panel[g][t]
                panel[g][t] = here + total_of([coef[c][g] * rows[c][t] for c in range(STEP)])
        for h in range(span):
            root = lax.rsqrt(pivots[h])
            low = [jnp.where(sub + 8 * h >= c, coef[c][q + h], 0.0) for c in range(min(STEP, 8 * h + 8))]
            out.append([total_of([low[c] * rows[c][t] for c in range(len(low))]) * root for t in range(tiles)])
    return jnp.concatenate([jnp.concatenate(o, axis=1) for o in out], axis=0)


def transform_kernel(gram_ref, ens_ref, out_ref, packed):
    total = 8 * gram_ref.shape[0]
    half = total // 2
    places = turned(out_ref.shape[0])
    first_row = ens_ref.shape[2] - out_ref.shape[2]
    states = jnp.concatenate([ens_ref[s, :, first_row:] for s in places], axis=0).astype(F32)
    mean_state = jnp.sum(states, axis=0, keepdims=True) / total
    anomalies = (states - mean_state).astype(BF16)
    row = lax.broadcasted_iota(jnp.int32, (total, total), 0)
    col = lax.broadcasted_iota(jnp.int32, (total, total), 1)
    for i in range(total // 8):
        for r in range(8):
            packed[8 * i + r : 8 * i + r + 1, :] = gram_ref[i, :, 128 * r : 128 * (r + 1)]
    diagonal, *cross = [gram_ref[i, :, 1024:] for i in range(3)]
    cross = jnp.concatenate(cross, axis=1)
    block, mixed = packed[:half], packed[half:]
    flipped = mixed.T
    above = (row < col)[:half, :half]
    below = (row > col)[:half, :half]
    first = jnp.where(above, flipped, mixed)
    second = jnp.where(above, mixed, jnp.where(below, flipped, diagonal))
    full = jnp.concatenate(
        [jnp.concatenate([first, block.T], axis=1), jnp.concatenate([block, second], axis=1)], axis=0
    )
    full = full + jnp.where(row == col, 1.0, 0.0)
    count = total // WIDE
    blocks = [full[WIDE * t : WIDE * (t + 1), :] for t in range(count)]
    weight = jnp.zeros((1, total), F32)
    for s in range(count):
        r0, r1 = WIDE * s, WIDE * (s + 1)
        done = eliminate([blocks[s][8 * g : 8 * (g + 1), :] for g in range(WIDE // 8)], r0)
        here = col[r0:r1]
        blocks[s] = jnp.where(here <= row[r0:r1], done, 0.0)
        if r1 < total:
            kept = jnp.where((here < r1) & (here > row[r0:r1]), 0.0, done)
            flipped = done.T
            inside = (here >= r0) & (here < r1)
            for t in range(s + 1, count):
                change = jnp.dot(flipped[WIDE * t : WIDE * (t + 1), :], kept, precision=HIGHEST, preferred_element_type=F32)
                blocks[t] = jnp.where(inside, 0.0, blocks[t]) - change
        solved = jnp.sum(blocks[s] * cross, axis=1, keepdims=True)
        weight = weight + jnp.sum(blocks[s] * solved, axis=0, keepdims=True)
    transposed = (jnp.concatenate(blocks, axis=0) + weight).astype(BF16)
    change = jnp.dot(transposed, anomalies, preferred_element_type=F32)
    result = (mean_state + change).astype(BF16)
    members = out_ref.shape[1]
    for i, s in enumerate(places):
        out_ref[s] = result[members * i : members * (i + 1)]


def transform(gram_sum, shared, width):
    sources, members = shared.shape[:2]
    return pl.pallas_call(
        transform_kernel,
        out_shape=jax.ShapeDtypeStruct((sources, members, width), BF16),
        scratch_shapes=[pltpu.VMEM((sources * members, sources * members // 2), F32)],
        compiler_params=pltpu.CompilerParams(vmem_limit_bytes=16 * 2**20),
    )(gram_sum, shared)


def to_all(x, axes, count):
    return lax.all_to_all(jnp.broadcast_to(x[None], (count,) + x.shape), axes, 0, 0, tiled=True)


def local(ensemble, operator_blocks, block_columns, observed, error_scale):
    ens_t = ensemble.T
    members, rows = ens_t.shape
    space_count = lax.axis_size(SPACE)
    member_count = lax.axis_size(MEMBER)
    plane_count = lax.axis_size(PLANE)
    z_count = lax.axis_size("z")
    total = members * member_count
    space_index = lax.axis_index(SPACE)
    left = lax.ppermute(ens_t[:, -128:], SPACE, [(i, (i + 1) % space_count) for i in range(space_count)])
    right = lax.ppermute(ens_t[:, :128], SPACE, [((i + 1) % space_count, i) for i in range(space_count)])
    state = jnp.pad(ens_t, ((0, 0), (128, 128)))
    state_local = rows // 128
    cols = jnp.mod(block_columns - space_index * state_local + 1, state_local * space_count)
    inverse = 1.0 / (error_scale * math.sqrt(total - 1))
    scaled, inverse = (observed * inverse).reshape(-1, 128), inverse.reshape(-1, 128)
    place = lax.axis_index(EXCHANGE).astype(jnp.int32).reshape(1)
    shared, side = predict(place, cols, state, left, right, scaled, inverse, operator_blocks, member_count)
    shared = lax.all_to_all(shared, EXCHANGE, 0, 0, tiled=True)
    part = gram(side, shared)
    part = jnp.sum(lax.all_to_all(part, PLANE, 0, 0, tiled=True), axis=0)
    part = jnp.sum(to_all(part, "z", z_count), axis=0)
    gram_sum = to_all(part, PLANE, plane_count).reshape(plane_count, 1, -1)
    analysis = lax.all_to_all(transform(gram_sum, shared, rows // member_count), EXCHANGE, 0, 0, tiled=True)
    return analysis.transpose(1, 0, 2).reshape(members, rows).T


def solution(mesh):
    fine = Mesh(mesh.devices.reshape(16, 2, 4, 4), ("z", "core", "y", "x"))
    in_specs = (P(SPACE, MEMBER), P(SPACE, None, None, None), P(SPACE, None), P(SPACE), P(SPACE))
    return jax.shard_map(local, mesh=fine, in_specs=in_specs, out_specs=P(SPACE, MEMBER), check_vma=False)
```
